32 devices in a mesh: section: 2 (over core), dp: 16 (over z, y, x).
Axes of the slice: x: 2, y: 2, z: 4, core: 2. Of those that a mesh axis runs over, the one named last changes fastest.
Arguments:
- flow_maps: float32 [192, 169, 512], P('dp'), may hold values from -6 to 6
- weights: float32 [2, 4608, 512], P('section'), may hold values from -0.09375 to 0.09375
- biases: float32 [2, 512], P('section'), may hold values from -3 to 3
- stack_lengths: int32 [192], P('dp'), may hold values from 5 to 10, as said below
- grad_seeds: int32 [192], P('dp'), may hold values from 0 to 65520
Outputs:
- conv5_act: float32 [192, 169, 512], P('dp', None, 'section')
- input_grad: float32 [192, 169, 512], P('dp', None, 'section')
- weight_grads: float32 [2, 4608, 512], P('section')
- bias_grads: float32 [2, 512], P('section')
The draws below stay inside these ranges and needn't reach their ends.
Inputs may be any that keep to these rules, and one draw needn't show every extreme that they name: `stack_lengths`: every length is 5 or 10, each taken by exactly half of all items.
All inputs are finite; a program needn't handle non-finite values.
Results may differ from the reference program's by a relative error of at most 0.0003.
Values sent between devices are 32-bit elements; how exact they have to be, the bound alone decides.
A program may use at most 320 MiB of HBM per device.

```python
import jax
import jax.numpy as jnp
from jax import lax

CH = 512
SIDE = 13
MICRO = 6
BATCH = 2
MAP = 169
KDIM = 4608
ITEMS = 192
N_DP = 16


def draw_stack_lengths(key, part):
    key = jax.random.fold_in(key, 3)
    order = jax.random.permutation(key, ITEMS)
    return (5 + 5 * (order % 2)).astype(jnp.int32)


def place_ends(values, stream_key, low, high):
    longest = values.shape.index(max(values.shape))
    spots = []
    for shift in (0, 1):
        where = [jax.random.randint(jax.random.fold_in(stream_key, axis), (), 0, length) for axis, length in enumerate(values.shape)]
        where[longest] = (where[longest] + shift) % values.shape[longest]
        spots.append(tuple(where))
    return values.at[spots[0]].set(low).at[spots[1]].set(high)


def block_scale(stream_key, shape, split, smallest, largest):
    def one(position, parts):
        heights = jax.random.uniform(jax.random.fold_in(jax.random.fold_in(stream_key, 6), position), (parts,), jnp.float32, smallest / len(split), largest / len(split))
        return jnp.repeat(jnp.exp(heights), shape[position] // parts).reshape((-1,) + (1,) * (len(shape) - position - 1))

    factor_of = one(*split[0])
    for cut in split[1:]:
        factor_of = factor_of * one(*cut)
    return factor_of


def centred(rng, dims, width, bound, split=(), kind=jnp.bfloat16):
    entries = jax.random.normal(rng, dims, jnp.float32) * width
    if len(split) > 0:
        entries = block_scale(rng, dims, split, -0.22, 0.18) * entries
    return jnp.clip(entries, min=-bound, max=bound).astype(kind)


def setup_inputs(seed: int = 0) -> dict:
    arg_keys = jax.random.split(jax.random.key(seed), 6)
    return {
        "flow_maps": centred(arg_keys[0], (ITEMS, MAP, CH), 1.0, 6.0, ((0, 16),), jnp.float32),
        "weights": centred(arg_keys[1], (2, KDIM, CH), KDIM ** -0.5, 0.09375, ((0, 2),), jnp.float32),
        "biases": centred(arg_keys[2], (2, CH), 0.5, 3.0, ((0, 2),), jnp.float32),
        "stack_lengths": draw_stack_lengths(jax.random.fold_in(arg_keys[5], 71), 0),
        "grad_seeds": place_ends(jax.random.randint(arg_keys[4], (ITEMS,), 0, 65521), jax.random.fold_in(arg_keys[4], 1), 0, 65520).astype(jnp.int32),
    }


def convolve(feature, matrix, offset_row):
    item_count = feature.shape[0]
    images = feature.reshape(item_count, SIDE, SIDE, CH)
    kernel = matrix.reshape(3, 3, CH, CH)
    result = lax.conv_general_dilated(images, kernel, (1, 1), ((1, 1), (1, 1)), dimension_numbers=('NHWC', 'HWIO', 'NHWC'), precision=lax.Precision.HIGHEST)
    return result.reshape(item_count, MAP, CH) + offset_row[None, None, :]

def forward(feature, weights, biases):
    hidden = jax.nn.silu(convolve(feature, weights[0], biases[0]))
    return jax.nn.silu(convolve(hidden, weights[1], biases[1]))

def upstream(seed_rows, lengths, channels, pixels):
    flat_index = jnp.arange(channels * pixels, dtype=jnp.int32)
    spread = flat_index * 7919 % 65521
    factor = seed_rows % 251 + 2
    hashed = (spread[None, :] * factor[:, None] + seed_rows[:, None]) % 65521
    values = hashed.astype(jnp.float32) / 32760.0 - 1.0
    scaled = values * (lengths.astype(jnp.float32) / 10.0)[:, None]
    return scaled.reshape(seed_rows.shape[0], pixels, channels)

def reference(flow_maps, weights, biases, stack_lengths, grad_seeds):
    group = MICRO * BATCH
    blocks = (flow_maps.reshape(N_DP, group, MAP, CH), stack_lengths.reshape(N_DP, group), grad_seeds.reshape(N_DP, group))

    def advance(carry, block):
        feature, lengths, seed_rows = block
        output, pull = jax.vjp(forward, feature, weights, biases)
        grads = pull(upstream(seed_rows, lengths, CH, MAP))
        return ((carry[0] + grads[1], carry[1] + grads[2]), (output, grads[0]))
    initial = (jnp.zeros((2, KDIM, CH), jnp.float32), jnp.zeros((2, CH), jnp.float32))
    totals, results = lax.scan(advance, initial, blocks)
    outputs, input_grads = results
    return (outputs.reshape(ITEMS, MAP, CH), input_grads.reshape(ITEMS, MAP, CH), totals[0], totals[1])
```

```python
import jax
import jax.numpy as jnp
from jax import lax
from jax.sharding import PartitionSpec as P

SIDE = 13


def conv(v, w):
    return lax.conv_general_dilated(
        v,
        w,
        (1, 1),
        ((1, 1), (1, 1)),
        dimension_numbers=("NHWC", "HWIO", "NHWC"),
        precision=lax.Precision.HIGH,
    )


def kernel_grad(v, d):
    return lax.conv_general_dilated(
        v,
        d,
        (1, 1),
        ((1, 1), (1, 1)),
        dimension_numbers=("CHWN", "IHWO", "HWNC"),
        precision=lax.Precision.HIGH,
    )


def back(d, w):
    flipped = w[::-1, ::-1]
    return lax.conv_general_dilated(
        d,
        flipped,
        (1, 1),
        ((1, 1), (1, 1)),
        dimension_numbers=("NHWC", "HWOI", "NHWC"),
        precision=lax.Precision.HIGH,
    )


def upstream(seed_rows, lengths, channels, pixels, first, count):
    flat_index = (
        jnp.arange(pixels, dtype=jnp.int32)[:, None] * channels
        + first
        + jnp.arange(count, dtype=jnp.int32)[None, :]
    )
    spread = flat_index * 7919 % 65521
    factor = (seed_rows % 251 + 2)[:, None, None]
    hashed = (spread[None] * factor + seed_rows[:, None, None]) % 65521
    values = hashed.astype(jnp.float32) / 32760.0 - 1.0
    return values * (lengths.astype(jnp.float32) / 10.0)[:, None, None]


def slope(z):
    s = jax.nn.sigmoid(z)
    return s * (1.0 + z * (1.0 - s))


def per_device(flow_maps, weights, biases, stack_lengths, grad_seeds):
    items, pixels, channels = flow_maps.shape
    half = channels // 2
    section = lax.axis_index("section")
    first = section * half
    both = lax.all_gather(weights[0], "section").reshape(2, 3, 3, channels, channels)
    both_bias = lax.all_gather(biases[0], "section")
    w4, w5 = both[0], both[1]

    def cols(w):
        return lax.dynamic_slice_in_dim(w, first, half, axis=3)

    def rows(w):
        return lax.dynamic_slice_in_dim(w, first, half, axis=2)

    def join(v):
        return lax.all_gather(v, "section", axis=3, tiled=True)

    x = flow_maps.reshape(items, SIDE, SIDE, channels)
    b4 = lax.dynamic_slice_in_dim(both_bias[0], first, half)
    b5 = lax.dynamic_slice_in_dim(both_bias[1], first, half)
    z4 = conv(x, cols(w4)) + b4
    hidden = join(jax.nn.silu(z4))
    z5 = conv(hidden, cols(w5)) + b5
    act = jax.nn.silu(z5)
    cot = upstream(grad_seeds, stack_lengths, channels, pixels, first, half)
    d5 = cot.reshape(z5.shape) * slope(z5)
    g5 = kernel_grad(hidden, d5)
    d4 = back(join(d5), rows(w5)) * slope(z4)
    g4 = kernel_grad(x, d4)
    gin = back(join(d4), rows(w4))
    gb = jnp.stack([d4.sum((0, 1, 2)), d5.sum((0, 1, 2))])
    g5 = lax.psum(g5, "dp")
    g4 = lax.psum(g4, "dp")
    gb = lax.psum(gb, "dp")
    is_first = section == 0
    mine = jnp.where(is_first, g4, g5)
    other = jnp.where(is_first, g5, g4)
    got = lax.ppermute(other, "section", [(0, 1), (1, 0)])
    mine, got = [v.reshape(9 * channels, half) for v in (mine, got)]
    wg = jnp.where(is_first, jnp.concatenate([mine, got], 1), jnp.concatenate([got, mine], 1))
    gb_all = lax.all_gather(gb, "section", axis=1, tiled=True)
    bg = jnp.where(is_first, gb_all[0], gb_all[1])
    return (
        act.reshape(items, pixels, half),
        gin.reshape(items, pixels, half),
        wg[None],
        bg[None],
    )


def solution(mesh):
    in_specs = (P("dp", None, None), P("section", None, None), P("section", None), P("dp"), P("dp"))
    out_specs = (
        P("dp", None, "section"),
        P("dp", None, "section"),
        P("section", None, None),
        P("section", None),
    )
    return jax.shard_map(
        per_device, mesh=mesh, in_specs=in_specs, out_specs=out_specs, check_vma=False
    )
```

```python
import functools

import jax
import jax.numpy as jnp
from jax import lax
from jax.experimental import pallas as pl
from jax.experimental.pallas import tpu as pltpu
from jax.sharding import PartitionSpec as P

SIDE = 13
PRIME = 65521
F32, BF16 = jnp.float32, jnp.bfloat16
MESH = pl.DeviceIdType.MESH
HEAD = 16


def ceil_to(value, unit):
    return -(-value // unit) * unit


def split(v):
    hi = v.astype(BF16)
    return hi, (v - hi.astype(F32)).astype(BF16)


def dot(a, b):
    return jnp.dot(a, b, preferred_element_type=F32)


def dot_nt(a, b):
    return lax.dot_general(a, b, (((1,), (1,)), ((), ())), preferred_element_type=F32)


def dot_tn(a, b):
    return lax.dot_general(a, b, (((0,), (0,)), ((), ())), preferred_element_type=F32)


def modulo(v):
    quotient = jnp.floor(v * (1.0 / PRIME) - 1e-4)
    rest = v - quotient * PRIME
    return jnp.where(rest >= PRIME, rest - PRIME, rest)


def clear_margins(staged, items, pitch):
    zeros = jnp.zeros((SIDE, HEAD, staged.shape[2]), F32)
    staged[:, 0:HEAD, :] = zeros
    staged[:, HEAD + pitch : HEAD + pitch + HEAD, :] = zeros


def clear_edges(taps):
    zeros = jnp.zeros(taps.shape[:2] + taps.shape[3:], BF16)
    taps[:, :, 0] = zeros
    taps[:, :, SIDE + 1] = zeros


def build_taps(staged, taps, items, pitch):
    @pl.loop(0, SIDE)
    def _(row):
        for col in range(3):
            start = HEAD + (col - 1) * items
            hi, lo = split(staged[row, start : start + pitch, :])
            taps[col, 0, row + 1] = hi
            taps[col, 1, row + 1] = lo


def window(taps, col, term, row):
    piece = taps[col, term, pl.ds(row, SIDE)]
    return piece.reshape(piece.shape[0] * piece.shape[1], piece.shape[2])


def each_tile(body, count=4):
    whole = SIDE // count

    @pl.loop(0, whole)
    def _(k):
        body(k * count, count)

    if SIDE % count:
        body(whole * count, SIDE % count)


def sigmoid(z):
    return 1.0 / (1.0 + jnp.exp(-z))


def forward_kernel(
    items, pitch,
    seeds, lengths, x_hbm, w_hbm, b_hbm,
    act_out, z4_out, d5_out, h0_out, x0_out, wr_out,
    fx, fh, tap_a, tap_b, tap_c, wstage, wbf, acc, bias, base,
    x_sem, wl_sem, ws_sem, wr_sem, row_sem, h_sem, b_sem, o_sem,
):
    section = lax.axis_index("section")
    other = 1 - section
    partner = {"section": other}
    half = acc.shape[2]
    taps3 = 3 * 2 * half
    barrier = pltpu.get_barrier_semaphore()
    pl.semaphore_signal(barrier, inc=1, device_id=partner, device_id_type=MESH)

    def mine(width):
        return pl.ds(pl.multiple_of(section * width, width), width)

    def theirs(width):
        return pl.ds(pl.multiple_of(other * width, width), width)

    x_copies = [
        pltpu.make_async_copy(
            x_hbm.at[:, :, pl.ds(h * half, half)],
            fx.at[h, :, pl.ds(HEAD, pitch)],
            x_sem.at[h],
        )
        for h in range(2)
    ]
    for copy in x_copies:
        copy.start()
    w_local, w_remote = [], []
    for g in range(3):
        rows = pl.ds(g * taps3, taps3)
        w_local.append(
            pltpu.make_async_copy(
                w_hbm.at[0, rows, mine(half)], wstage.at[section, rows], wl_sem.at[g]
            )
        )
        w_remote.append(
            pltpu.make_async_remote_copy(
                w_hbm.at[0, rows, theirs(half)], wstage.at[section, rows],
                ws_sem.at[g], wr_sem.at[g], device_id=partner, device_id_type=MESH,
            )
        )
    for copy in w_local:
        copy.start()
    b_local = pltpu.make_async_copy(b_hbm, bias.at[section], b_sem.at[0])
    b_local.start()
    pl.semaphore_wait(barrier, 1)
    b_remote = pltpu.make_async_remote_copy(
        b_hbm, bias.at[section], b_sem.at[1], b_sem.at[2], device_id=partner, device_id_type=MESH
    )
    b_remote.start()
    for copy in w_remote:
        copy.start()
    rows_remote = pltpu.make_async_remote_copy(
        w_hbm.at[0].reshape(9, 2 * half, 2 * half).at[:, theirs(half)], wr_out,
        row_sem.at[0], row_sem.at[1], device_id=partner, device_id_type=MESH,
    )
    rows_remote.start()

    for taps in (tap_a, tap_b, tap_c):
        clear_edges(taps)
    for h in range(2):
        clear_margins(fx.at[h], items, pitch)
        clear_margins(fh.at[h], items, pitch)

    item_of = lax.broadcasted_iota(jnp.int32, (pitch, half), 0)
    column = jnp.floor((item_of.astype(F32) + 0.5) * (1.0 / items))
    item_row = item_of.astype(F32) - column * items
    seed_rows = jnp.zeros((pitch, half), F32)
    factor_rows = jnp.zeros((pitch, half), F32)
    scale_rows = jnp.zeros((pitch, half), F32)
    for n in range(items):
        hit = item_row == float(n)
        seed = seeds[n]
        seed_rows = jnp.where(hit, seed.astype(F32), seed_rows)
        factor_rows = jnp.where(hit, (seed % 251 + 2).astype(F32), factor_rows)
        scale_rows = jnp.where(hit, lengths[n].astype(F32) / 10.0, scale_rows)
    channel = lax.broadcasted_iota(jnp.int32, (pitch, half), 1) + section * half
    per_pixel = 7919 * 2 * half % PRIME
    base[0] = modulo(column * per_pixel + channel.astype(F32) * 7919.0)
    base[1] = seed_rows
    base[2] = factor_rows
    base[3] = scale_rows
    real = base.at[4]
    real[...] = jnp.where(item_of < items * SIDE, 1.0, 0.0)

    out_copies = []
    for h, taps in ((0, tap_a), (1, tap_b)):
        x_copies[h].wait()
        build_taps(fx.at[h], taps, items, pitch)
        copy = pltpu.make_async_copy(taps.at[1, :, pl.ds(1, SIDE)], x0_out.at[h], o_sem.at[h])
        copy.start()
        out_copies.append(copy)
    b_local.wait()
    b_remote.wait()

    def weights_ready(layer, g):
        @pl.when(section == layer)
        def _():
            w_local[g].wait()

        @pl.when(section != layer)
        def _():
            w_remote[g].wait_recv()

        @pl.loop(0, 3)
        def _(k):
            t = g * 3 + k
            hi, lo = split(wstage[layer, pl.ds(pl.multiple_of(t * 2 * half, 2 * half), 2 * half), :])
            wbf[0, t] = hi
            wbf[1, t] = lo

    def product(parts, first):
        def tile(start, count):
            total = None
            for taps, t, rows in parts:
                row, col = t // 3, t % 3
                for a, b in ((0, 0), (1, 0), (0, 1)):
                    v = taps[col, a, pl.ds(start + row, count)].reshape(count * pitch, half)
                    term = dot(v, wbf[b, t, rows, :])
                    total = term if total is None else total + term
            total = total.reshape(count, pitch, half)
            where = pl.ds(start, count)
            acc[where] = total if first else acc[where] + total

        each_tile(tile)

    for g in range(3):
        weights_ready(0, g)
        product(
            [
                (taps, g * 3 + k, slice(h * half, (h + 1) * half))
                for h, taps in ((0, tap_a), (1, tap_b))
                for k in range(3)
            ],
            g == 0,
        )

    my_half = mine(half)
    bias4 = bias[0, :, my_half]

    @pl.loop(0, SIDE)
    def _(row):
        z = acc[row] + bias4
        fx[0, row, pl.ds(HEAD, pitch)] = z
        fh[0, row, pl.ds(HEAD, pitch)] = z * sigmoid(z) * real[...]

    h_remote = pltpu.make_async_remote_copy(
        fh.at[0, :, pl.ds(HEAD, pitch)], fh.at[1, :, pl.ds(HEAD, pitch)],
        h_sem.at[0], h_sem.at[1], device_id=partner, device_id_type=MESH,
    )
    h_remote.start()
    copy = pltpu.make_async_copy(fx.at[0, :, pl.ds(HEAD, pitch)], z4_out, o_sem.at[2])
    copy.start()
    out_copies.append(copy)
    build_taps(fh.at[0], tap_c, items, pitch)
    copy = pltpu.make_async_copy(tap_c.at[1, :, pl.ds(1, SIDE)], h0_out.at[section], o_sem.at[3])
    copy.start()
    out_copies.append(copy)
    for g in range(3):
        weights_ready(1, g)
    product([(tap_c, t, my_half) for t in range(9)], True)
    h_remote.wait_recv()
    out_copies[0].wait()
    build_taps(fh.at[1], tap_a, items, pitch)
    copy = pltpu.make_async_copy(tap_a.at[1, :, pl.ds(1, SIDE)], h0_out.at[other], o_sem.at[0])
    copy.start()
    out_copies[0] = copy
    product([(tap_a, t, theirs(half)) for t in range(9)], False)
    bias5 = bias[1, :, my_half]
    for copy in out_copies:
        copy.wait()
    h_remote.wait_send()

    @pl.loop(0, SIDE)
    def _(row):
        z = acc[row] + bias5
        s = sigmoid(z)
        fx[0, row, pl.ds(HEAD, pitch)] = z * s
        shift = (row * (per_pixel * SIDE)) % PRIME
        a = base[0] + shift.astype(F32)
        a = jnp.where(a >= PRIME, a - PRIME, a)
        hashed = modulo(a * base[2] + base[1])
        cotangent = (hashed / 32760.0 - 1.0) * base[3] * real[...]
        fx[1, row, pl.ds(HEAD, pitch)] = cotangent * (s * (1.0 + z * (1.0 - s)))

    last = [
        pltpu.make_async_copy(fx.at[0, :, pl.ds(HEAD, pitch)], act_out, o_sem.at[0]),
        pltpu.make_async_copy(fx.at[1, :, pl.ds(HEAD, pitch)], d5_out, o_sem.at[1]),
    ]
    for copy in last:
        copy.start()
    for copy in w_remote:
        copy.wait_send()
    rows_remote.wait()
    for copy in last:
        copy.wait()


def forward(x, weights, biases, seeds, lengths, items, pitch):
    channels = x.shape[2]
    half = channels // 2
    maps = (SIDE, pitch, half)
    any_spec = pl.BlockSpec(memory_space=pl.ANY)
    smem = pl.BlockSpec(memory_space=pltpu.SMEM)
    taps = pltpu.VMEM((3, 2, SIDE + 2, pitch, half), BF16)
    staged = pltpu.VMEM((2, SIDE, HEAD + pitch + HEAD, half), F32)
    dma = pltpu.SemaphoreType.DMA
    terms = jax.ShapeDtypeStruct((2, 2) + maps, BF16)
    one = jax.ShapeDtypeStruct(maps, F32)
    return pl.pallas_call(
        functools.partial(forward_kernel, items, pitch),
        name="forward",
        out_shape=[one, one, one, terms, terms, jax.ShapeDtypeStruct((9, half, channels), F32)],
        in_specs=[smem, smem, any_spec, any_spec, any_spec],
        out_specs=[any_spec] * 6,
        scratch_shapes=[
            staged, staged, taps, taps, taps,
            pltpu.VMEM((2, 9 * channels, half), F32),
            pltpu.VMEM((2, 9, channels, half), BF16),
            pltpu.VMEM(maps, F32),
            pltpu.VMEM((2, 1, channels), F32),
            pltpu.VMEM((5, pitch, half), F32),
            dma((2,)), dma((3,)), dma((3,)), dma((3,)), dma((2,)), dma((2,)), dma((3,)), dma((4,)),
        ],
        compiler_params=pltpu.CompilerParams(
            collective_id=0, has_side_effects=True, vmem_limit_bytes=62 * 2**20
        ),
    )(seeds, lengths, x, weights, biases)


RING = 24


def exchange(n, own, r_first, r_line, r_last, fin, gx, wg, sems):
    (f_s, f_r, z_s, z_r, l_s, l_r, a_s, a_r, c_s, g_s, g_r, p_s, p_r) = sems
    half = own.shape[1]
    part, chunk = half // 2, half // 8
    units = gx.shape[1] // half
    section, dp = lax.axis_index("section"), lax.axis_index("dp")
    x, y, z = dp % 2, dp // 2 % 2, dp // 4
    kind, slot = n % 2, n % RING
    layer, row0 = 1 - n // units, n % units * half
    keep = (1 - kind) * x + kind * y
    to_x, to_y = dp + 1 - 2 * x, dp + 2 - 4 * y
    first = {"dp": (1 - kind) * to_x + kind * to_y}
    last = {"dp": kind * to_x + (1 - kind) * to_y}
    up = {"dp": dp + 4 - 8 * (z // 3)}
    down = {"dp": dp - 4 + 8 * ((3 - z) // 3)}

    def rows(start, size):
        return pl.ds(pl.multiple_of(start, chunk), size)

    def remote(src, dst, send, recv, device):
        return pltpu.make_async_remote_copy(
            src, dst, send, recv, device_id=device, device_id_type=MESH
        )

    base = keep * part

    def first_copy():
        src = own.at[slot, rows((1 - keep) * part, part)]
        return remote(src, r_first.at[slot], f_s.at[slot], f_r.at[slot], first)

    def line(way, lo, count):
        return remote(
            own.at[slot, rows(base + lo * chunk, count * chunk)],
            r_line.at[slot, way, pl.ds(lo * chunk, count * chunk)],
            z_s.at[slot, way], z_r.at[slot, way], (up, down)[way],
        )

    def line_add(way, lo, count):
        line(way, lo, count).wait_recv()
        where = rows(base + lo * chunk, count * chunk)
        own[slot, where] += r_line[slot, way, pl.ds(lo * chunk, count * chunk)]

    def last_copy():
        src = own.at[slot, rows(base + z * chunk, chunk)]
        return remote(src, r_last.at[slot], l_s.at[slot], l_r.at[slot], last)

    columns = pl.ds(pl.multiple_of(section * half, half), half)

    def home(body):
        @pl.when(layer == section)
        def _():
            body(lambda start, size: wg.at[rows(row0 + start, size), columns])

        @pl.when(layer != section)
        def _():
            body(lambda start, size: gx.at[layer, rows(row0 + start, size)])

    def place(where, j):
        return where(base + j * chunk, chunk)

    def spread(where, j, way, src=None):
        src = place(where, j) if src is None else src
        return remote(src, place(where, j), a_s.at[slot, j, way], a_r.at[slot, j], (up, down)[way])

    def keep_copy(where):
        return pltpu.make_async_copy(fin.at[slot], place(where, z), c_s.at[slot])

    def back_copy(where):
        kept = where(base, part)
        return remote(kept, kept, g_s.at[slot], g_r.at[slot], first)

    def put_remote():
        unit, target = gx.at[layer, rows(row0, half)], wg.at[rows(row0, half), columns]
        return remote(unit, target, p_s.at[slot], p_r.at[slot], {"section": 1 - section})

    def stage0():
        first_copy().start()

    def stage1():
        first_copy().wait_recv()
        own[slot, rows(base, part)] += r_first[slot]
        pl.when(z == 0)(lambda: line(0, 1, 3).start())
        pl.when(z == 3)(lambda: line(1, 0, 3).start())

    def stage2():
        @pl.when(z == 1)
        def _():
            line_add(0, 1, 3)
            line(0, 2, 2).start()

        @pl.when(z == 2)
        def _():
            line_add(1, 0, 3)
            line(1, 0, 2).start()

    def stage3():
        @pl.when(z == 1)
        def _():
            line_add(1, 0, 2)
            line(1, 0, 1).start()

        @pl.when(z == 2)
        def _():
            line_add(0, 2, 2)
            line(0, 3, 1).start()

    def stage4():
        pl.when(z == 0)(lambda: line_add(1, 0, 1))
        pl.when(z == 3)(lambda: line_add(0, 3, 1))
        last_copy().start()

    def stage5():
        last_copy().wait_recv()
        fin[slot] = own[slot, rows(base + z * chunk, chunk)] + r_last[slot]

        def body(where):
            keep_copy(where).start()
            pl.when(z < 3)(lambda: spread(where, z, 0, fin.at[slot]).start())
            pl.when(z > 0)(lambda: spread(where, z, 1, fin.at[slot]).start())

        home(body)

    def passing(k):
        def body(where):
            @pl.when(z >= k)
            def _():
                spread(where, z - k, 0).wait_recv()
                pl.when(z < 3)(lambda: spread(where, z - k, 0).start())

            @pl.when(z + k <= 3)
            def _():
                spread(where, z + k, 1).wait_recv()
                pl.when(z > 0)(lambda: spread(where, z + k, 1).start())

        home(body)

    def stage8():
        passing(3)

        def body(where):
            keep_copy(where).wait()
            back_copy(where).start()

        home(body)

    def stage9():
        home(lambda where: back_copy(where).wait_recv())
        pl.when(layer != section)(lambda: put_remote().start())

    def stage10():
        pl.when(layer == section)(lambda: put_remote().wait_recv())
        pl.when(layer != section)(lambda: put_remote().wait_send())
        first_copy().wait_send()
        last_copy().wait_send()
        for k in range(4):
            pl.when(z == k)(lambda k=k: line(0, k + 1, 3 - k).wait_send() if k < 3 else None)
            pl.when(z == k)(lambda k=k: line(1, 0, k).wait_send() if k > 0 else None)

        def body(where):
            back_copy(where).wait_send()
            for k in range(4):
                pl.when((z < 3) & (z >= k))(lambda k=k: spread(where, k, 0).wait_send())
                pl.when((z > 0) & (z <= k))(lambda k=k: spread(where, k, 1).wait_send())

        home(body)

    return [
        stage0, stage1, stage2, stage3, stage4, stage5,
        lambda: passing(1), lambda: passing(2), stage8, stage9, stage10,
    ]


OFFSETS = (0, 5, 9, 12, 15, 19, 22, 25, 28, 33, 35)


def backward_kernel(
    items, pitch, reduce,
    d5_hbm, z4_hbm, h0_hbm, x0_hbm, w_hbm, wr_hbm,
    gin_out, gx_out, wg_out, bg_out,
    fd, taps, feature, z4, acc, wstage, own, r_first, r_line, r_last, fin, b_send, b_recv, b_row,
    l_sem, w_sem, d_sem, bs_sem, br_sem, bo_sem, *sems,
):
    section, dp = lax.axis_index("section"), lax.axis_index("dp")
    other = 1 - section
    partner = {"section": other}
    half = acc.shape[2]
    rows_all = SIDE * pitch
    units = 18
    x, y, z = dp % 2, dp // 2 % 2, dp // 4
    pairs = [{"dp": dp + 1 - 2 * x}, {"dp": dp + 2 - 4 * y}]
    pairs += [{"dp": dp + 4 - 8 * (z % 2)}, {"dp": dp + 8 - 16 * (z // 2)}]
    barrier = pltpu.get_barrier_semaphore()

    def greet(device):
        pl.semaphore_signal(barrier, inc=1, device_id=device, device_id_type=MESH)

    greet(partner)
    if reduce:
        for device in pairs:
            greet(device)
        pl.when(z == 1)(lambda: greet({"dp": dp + 4}))
        pl.when(z == 2)(lambda: greet({"dp": dp - 4}))

    def mine(width):
        return pl.ds(pl.multiple_of(section * width, width), width)

    d_local = pltpu.make_async_copy(d5_hbm, fd.at[0, :, pl.ds(HEAD, pitch)], l_sem.at[0])
    h_local = pltpu.make_async_copy(h0_hbm, feature.at[1], l_sem.at[1])
    z_local = pltpu.make_async_copy(z4_hbm, z4, l_sem.at[2])
    x_local = pltpu.make_async_copy(x0_hbm, feature.at[0], l_sem.at[3])
    for copy in (d_local, h_local, z_local, x_local):
        copy.start()

    def w_copy(n, act):
        layer, step = 1 - n // units, n % units
        t = step % 9
        column = (section + step // 9) % 2 * half
        columns = pl.ds(pl.multiple_of(column, half), half)
        slot = n % 2
        whole = w_hbm.at[0].reshape(9, 2 * half, 2 * half)

        @pl.when(layer == section)
        def _():
            copy = pltpu.make_async_copy(
                whole.at[t, mine(half), columns], wstage.at[slot], w_sem.at[slot]
            )
            act(copy)

        @pl.when(layer != section)
        def _():
            act(pltpu.make_async_copy(wr_hbm.at[t, :, columns], wstage.at[slot], w_sem.at[slot]))

    w_copy(0, lambda copy: copy.start())
    for k in range(3):
        clear_margins(fd.at[k], items, pitch)
    for k in range(2):
        clear_edges(taps.at[k])
    pl.semaphore_wait(barrier, 5 + (z + 1) // 2 % 2 if reduce else 1)

    def d_remote(k):
        src = d5_hbm if k == 0 else fd.at[0, :, pl.ds(HEAD, pitch)]
        return pltpu.make_async_remote_copy(
            src, fd.at[1 + k, :, pl.ds(HEAD, pitch)],
            d_sem.at[k, 0], d_sem.at[k, 1], device_id=partner, device_id_type=MESH,
        )

    d_remote(0).start()
    real = lax.broadcasted_iota(jnp.int32, (pitch, half), 0) < items * SIDE

    def column_sums():
        def add(row, total):
            v = fd[0, row, pl.ds(HEAD, pitch)]
            return total + jnp.sum(v.reshape(pitch // 8, 8, half), axis=0)

        return jnp.sum(lax.fori_loop(0, SIDE, add, jnp.zeros((8, half), F32)), axis=0, keepdims=True)

    d_local.wait()
    build_taps(fd.at[0], taps.at[0], items, pitch)
    b_send[0, 0:8] = jnp.broadcast_to(column_sums(), (8, half))
    acc[...] = jnp.zeros_like(acc)
    h_local.wait()

    def enter(layer):
        z_local.wait()
        x_local.wait()

        @pl.loop(0, SIDE)
        def _(row):
            v = z4[row]
            s = sigmoid(v)
            d = acc[row] * (s * (1.0 + v * (1.0 - s)))
            fd[0, row, pl.ds(HEAD, pitch)] = jnp.where(real, d, 0.0)

        d_remote(1).start()
        build_taps(fd.at[0], taps.at[0], items, pitch)
        which = lax.broadcasted_iota(jnp.int32, (8, half), 0) == 0
        b_send[0] = jnp.where(which, jnp.broadcast_to(column_sums(), (8, half)), b_send[0])
        acc[...] = jnp.zeros_like(acc)

    def receive(k):
        d_remote(k).wait_recv()
        build_taps(fd.at[1 + k], taps.at[1], items, pitch)

    def kernel_unit(n):
        layer, step = 1 - n // units, n % units
        t, m = step // 2, step % 2
        row, col = 2 - t // 3, 2 - t % 3
        v = [feature[layer, m, term].reshape(rows_all, half) for term in range(2)]
        d = [window(taps.at[0], col, term, row) for term in range(2)]
        terms = ((0, 0), (1, 0), (0, 1))
        tail = rows_all % 256
        cut = rows_all - tail if 3 * tail <= 256 else rows_all
        total = None
        for a, b in terms:
            part = dot_tn(v[a][:cut], d[b][:cut])
            total = part if total is None else total + part
        if cut < rows_all:
            total += dot_tn(
                jnp.concatenate([v[a][cut:] for a, b in terms], 0),
                jnp.concatenate([d[b][cut:] for a, b in terms], 0),
            )
        own[n % RING] = total

    def input_piece(n):
        w_copy(n, lambda copy: copy.wait())
        pl.when(n + 1 < 2 * units)(lambda: w_copy(n + 1, lambda copy: copy.start()))
        step = n % units
        h, t = step // 9, step % 9
        row, col = 2 - t // 3, 2 - t % 3
        w = split(wstage[n % 2])

        def tile(start, count):
            total = None
            for a, b in ((0, 0), (1, 0), (0, 1)):
                v = taps[h, col, a, pl.ds(start + row, count)].reshape(count * pitch, half)
                part = dot_nt(v, w[b])
                total = part if total is None else total + part
            acc[pl.ds(start, count)] += total.reshape(count, pitch, half)

        each_tile(tile)

    def bias_copy(k, device):
        return pltpu.make_async_remote_copy(
            b_send.at[k], b_recv.at[k], bs_sem.at[k], br_sem.at[k], device_id=device, device_id_type=MESH
        )

    def bias_step(k):
        if reduce and k > 0:
            bias_copy(k - 1, pairs[k - 1]).wait_recv()
            b_send[k] = b_send[k - 1] + b_recv[k - 1]
        if reduce and k < 4:
            bias_copy(k, pairs[k]).start()
        if k == 4 and not reduce:
            b_send[4] = b_send[0]
        if k == 4:
            pltpu.make_async_copy(b_send.at[4], bg_out, bo_sem.at[0]).start()

    put_acc = pltpu.make_async_copy(acc, gin_out, l_sem.at[4])

    def local_part(n):
        layer, row0 = 1 - n // units, n % units * half
        dst = gx_out.at[layer, pl.ds(pl.multiple_of(row0, half), half)]
        return pltpu.make_async_copy(own.at[n % RING], dst, sems[0].at[n % RING])

    def service(u, odd):
        for k, offset in enumerate(OFFSETS):
            if k == 0 or offset % 2 != odd:
                continue
            n = u - offset // 2

            @pl.when((n >= 0) & (n < 2 * units))
            def _():
                stages = exchange(n, own, r_first, r_line, r_last, fin, gx_out, wg_out, sems)
                stages[k]()

    last = 2 * units + (OFFSETS[-1] + 1) // 2 if reduce else 2 * units

    @pl.loop(0, last)
    def _(u):
        busy = u < 2 * units
        pl.when((u == units // 2) | False)(lambda: receive(0))
        pl.when(u == units)(lambda: enter(0))
        pl.when(u == units + units // 2)(lambda: receive(1))

        @pl.when(busy)
        def _():
            if not reduce:
                pl.when(u >= RING)(lambda: local_part(u - RING).wait())
            kernel_unit(u)
            if reduce:
                exchange(u, own, r_first, r_line, r_last, fin, gx_out, wg_out, sems)[0]()
            else:
                local_part(u).start()

        if reduce:
            service(u, 0)
        pl.when(busy)(lambda: input_piece(u))
        pl.when(u == 2 * units - 1)(lambda: put_acc.start())
        if reduce:
            service(u, 1)
        for k in range(5):
            pl.when(u == units + 2 + 2 * k)(lambda k=k: bias_step(k))

    if not reduce:

        @pl.loop(2 * units - RING, 2 * units)
        def _(n):
            local_part(n).wait()

    for k in range(4 if reduce else 0):
        bias_copy(k, pairs[k]).wait_send()
    pltpu.make_async_copy(b_send.at[4], bg_out, bo_sem.at[0]).wait()
    for k in range(2):
        d_remote(k).wait_send()
    put_acc.wait()


def backward(d5, z4, h0, x0, weights, rows_other, items, reduce):
    maps = d5.shape
    _, pitch, half = maps
    channels = 2 * half
    any_spec = pl.BlockSpec(memory_space=pl.ANY)
    dma = pltpu.SemaphoreType.DMA
    shape = jax.ShapeDtypeStruct
    ring = RING
    part, chunk = half // 2, half // 8
    return pl.pallas_call(
        functools.partial(backward_kernel, items, pitch, reduce),
        name="backward",
        out_shape=[
            shape(maps, F32),
            shape((2, 9 * channels, half), F32),
            shape((9 * channels, channels), F32),
            shape((8, half), F32),
        ],
        in_specs=[any_spec] * 6,
        out_specs=[any_spec] * 4,
        scratch_shapes=[
            pltpu.VMEM((3, SIDE, HEAD + pitch + HEAD, half), F32),
            pltpu.VMEM((2, 3, 2, SIDE + 2, pitch, half), BF16),
            pltpu.VMEM((2, 2, 2) + maps, BF16),
            pltpu.VMEM(maps, F32),
            pltpu.VMEM(maps, F32),
            pltpu.VMEM((2, half, half), F32),
            pltpu.VMEM((ring, half, half), F32),
            pltpu.VMEM((ring, part, half), F32),
            pltpu.VMEM((ring, 2, part, half), F32),
            pltpu.VMEM((ring, chunk, half), F32),
            pltpu.VMEM((ring, chunk, half), F32),
            pltpu.VMEM((5, 8, half), F32),
            pltpu.VMEM((4, 8, half), F32),
            pltpu.VMEM((8, half), F32),
            dma((5,)), dma((2,)), dma((2, 2)), dma((4,)), dma((4,)), dma((1,)),
            dma((ring,)), dma((ring,)), dma((ring, 2)), dma((ring, 2)), dma((ring,)), dma((ring,)),
            dma((ring, 4, 2)), dma((ring, 4)), dma((ring,)), dma((ring,)), dma((ring,)),
            dma((ring,)), dma((ring,)),
        ],
        compiler_params=pltpu.CompilerParams(
            collective_id=1, has_side_effects=True, vmem_limit_bytes=62 * 2**20
        ),
    )(d5, z4, h0, x0, weights, rows_other)


def to_rows(maps, pitch):
    items, pixels, channels = maps.shape
    rows = maps.transpose(1, 0, 2).reshape(SIDE, pixels // SIDE * items, channels)
    return jnp.pad(rows, ((0, 0), (0, pitch - rows.shape[1]), (0, 0)))


def from_rows(rows, items):
    side, _, channels = rows.shape
    maps = rows[:, : side * items].reshape(side * side, items, channels)
    return maps.transpose(1, 0, 2)


def per_device(flow_maps, weights, biases, stack_lengths, grad_seeds):
    items = flow_maps.shape[0]
    channels = flow_maps.shape[2]
    half = channels // 2
    pitch = ceil_to(items * SIDE, 16)
    section = lax.axis_index("section")
    act, z4, d5, h0, x0, rows_other = forward(
        to_rows(flow_maps, pitch), weights, biases, grad_seeds, stack_lengths, items, pitch
    )
    fused = lax.axis_size("dp") == 16
    gin, parts, grad, bias = backward(d5, z4, h0, x0, weights, rows_other, items, fused)
    bias = bias[:2]
    if not fused:
        parts, bias = lax.psum((parts, bias), "dp")
        given = lax.dynamic_index_in_dim(parts, 1 - section, 0, keepdims=False)
        kept = lax.dynamic_index_in_dim(parts, section, 0, keepdims=False)
        got = lax.ppermute(given, "section", [(0, 1), (1, 0)])
        first, second = jnp.where(section == 0, kept, got), jnp.where(section == 0, got, kept)
        grad = jnp.concatenate([first, second], axis=1)
    both = lax.all_gather(bias, "section", axis=1, tiled=True)
    bias = lax.dynamic_index_in_dim(both, section, 0)
    return (from_rows(act, items), from_rows(gin, items), grad[None], bias)


def solution(mesh):
    in_specs = (P("dp", None, None), P("section", None, None), P("section", None), P("dp"), P("dp"))
    out_specs = (
        P("dp", None, "section"),
        P("dp", None, "section"),
        P("section", None, None),
        P("section", None),
    )
    return jax.shard_map(
        per_device, mesh=mesh, in_specs=in_specs, out_specs=out_specs, check_vma=False
    )
```

```python
import functools

import jax
import jax.numpy as jnp
from jax import lax
from jax.experimental import pallas as pl
from jax.experimental.pallas import tpu as pltpu
from jax.sharding import PartitionSpec as P

SIDE = 13
PRIME = 65521
F32, BF16 = jnp.float32, jnp.bfloat16
MESH = pl.DeviceIdType.MESH
LANES = 128
HEAD = 16


def ceil_to(value, unit):
    return -(-value // unit) * unit


def split(v):
    hi = v.astype(BF16)
    return hi, (v - hi.astype(F32)).astype(BF16)


def dot(a, b):
    return jnp.dot(a, b, preferred_element_type=F32)


def dot_nt(a, b):
    return lax.dot_general(a, b, (((1,), (1,)), ((), ())), preferred_element_type=F32)


def dot_tn(a, b):
    return lax.dot_general(a, b, (((0,), (0,)), ((), ())), preferred_element_type=F32)


def modulo(v):
    quotient = jnp.floor(v * (1.0 / PRIME) - 1e-4)
    rest = v - quotient * PRIME
    return jnp.where(rest >= PRIME, rest - PRIME, rest)


def clear_margins(staged, items, pitch):
    zeros = jnp.zeros((SIDE, HEAD, staged.shape[2]), F32)
    staged[:, 0:HEAD, :] = zeros
    staged[:, HEAD + pitch : HEAD + pitch + HEAD, :] = zeros


def clear_edges(taps):
    zeros = jnp.zeros(taps.shape[:2] + taps.shape[3:], BF16)
    taps[:, :, 0] = zeros
    taps[:, :, SIDE + 1] = zeros


def build_taps(staged, taps, items, pitch):
    @pl.loop(0, SIDE)
    def _(row):
        for col in range(3):
            start = HEAD + (col - 1) * items
            hi, lo = split(staged[row, start : start + pitch, :])
            taps[col, 0, row + 1] = hi
            taps[col, 1, row + 1] = lo


def gather_rows(maps, staged, items):
    for row in range(SIDE):
        for n in range(items):
            for tile in range(staged.shape[0]):
                staged[tile, row, pl.ds(HEAD + n, SIDE, stride=items), :] = maps[
                    n, row * SIDE : (row + 1) * SIDE, tile * LANES : (tile + 1) * LANES
                ]


def build_tiled(staged, taps, items, pitch):
    @pl.loop(0, SIDE)
    def _(row):
        for col in range(3):
            start = HEAD + (col - 1) * items
            for tile in range(staged.shape[0]):
                hi, lo = split(staged[tile, row, start : start + pitch, :])
                lanes = slice(tile * LANES, (tile + 1) * LANES)
                taps[col, 0, row + 1, :, lanes] = hi
                taps[col, 1, row + 1, :, lanes] = lo


def window(taps, col, term, row):
    piece = taps[col, term, pl.ds(row, SIDE)]
    return piece.reshape(piece.shape[0] * piece.shape[1], piece.shape[2])


def each_tile(body, count=4):
    whole = SIDE // count

    @pl.loop(0, whole)
    def _(k):
        body(k * count, count)

    if SIDE % count:
        body(whole * count, SIDE % count)


def sigmoid(z):
    return 1.0 / (1.0 + jnp.exp(-z))


def forward_kernel(
    items, pitch,
    seeds, lengths, x_hbm, w_hbm, b_hbm,
    act_out, z4_out, d5_out, h0_out, x0_out, wr_out,
    maps, fx, fh, tap_a, tap_b, tap_c, wstage, wbf, acc, bias, base,
    x_sem, wl_sem, ws_sem, wr_sem, row_sem, h_sem, b_sem, o_sem,
):
    section = lax.axis_index("section")
    other = 1 - section
    partner = {"section": other}
    half = acc.shape[2]
    taps3 = 3 * 2 * half
    barrier = pltpu.get_barrier_semaphore()
    pl.semaphore_signal(barrier, inc=1, device_id=partner, device_id_type=MESH)

    def mine(width):
        return pl.ds(pl.multiple_of(section * width, width), width)

    def theirs(width):
        return pl.ds(pl.multiple_of(other * width, width), width)

    x_copies = [
        pltpu.make_async_copy(
            x_hbm.at[:, :, pl.ds(h * half, half)], maps.at[:, :, pl.ds(h * half, half)], x_sem.at[h]
        )
        for h in range(2)
    ]
    for copy in x_copies:
        copy.start()
    w_local, w_remote = [], []
    for g in range(3):
        rows = pl.ds(g * taps3, taps3)
        w_local.append(
            pltpu.make_async_copy(
                w_hbm.at[0, rows, mine(half)], wstage.at[section, rows], wl_sem.at[g]
            )
        )
        w_remote.append(
            pltpu.make_async_remote_copy(
                w_hbm.at[0, rows, theirs(half)], wstage.at[section, rows],
                ws_sem.at[g], wr_sem.at[g], device_id=partner, device_id_type=MESH,
            )
        )
    for copy in w_local:
        copy.start()
    b_local = pltpu.make_async_copy(b_hbm, bias.at[section], b_sem.at[0])
    b_local.start()
    pl.semaphore_wait(barrier, 1)
    b_remote = pltpu.make_async_remote_copy(
        b_hbm, bias.at[section], b_sem.at[1], b_sem.at[2], device_id=partner, device_id_type=MESH
    )
    b_remote.start()
    for copy in w_remote:
        copy.start()
    rows_remote = pltpu.make_async_remote_copy(
        w_hbm.at[0].reshape(9, 2 * half, 2 * half).at[:, theirs(half)], wr_out,
        row_sem.at[0], row_sem.at[1], device_id=partner, device_id_type=MESH,
    )
    rows_remote.start()

    for taps in (tap_a, tap_b, tap_c):
        clear_edges(taps)
    tiles = half // LANES
    for tile in range(2 * tiles):
        fx[tile] = jnp.zeros(fx.shape[1:], F32)
    for h in range(2):
        clear_margins(fh.at[h], items, pitch)

    item_of = lax.broadcasted_iota(jnp.int32, (pitch, half), 0)
    column = jnp.floor((item_of.astype(F32) + 0.5) * (1.0 / items))
    item_row = item_of.astype(F32) - column * items
    seed_rows = jnp.zeros((pitch, half), F32)
    factor_rows = jnp.zeros((pitch, half), F32)
    scale_rows = jnp.zeros((pitch, half), F32)
    for n in range(items):
        hit = item_row == float(n)
        seed = seeds[n]
        seed_rows = jnp.where(hit, seed.astype(F32), seed_rows)
        factor_rows = jnp.where(hit, (seed % 251 + 2).astype(F32), factor_rows)
        scale_rows = jnp.where(hit, lengths[n].astype(F32) / 10.0, scale_rows)
    channel = lax.broadcasted_iota(jnp.int32, (pitch, half), 1) + section * half
    per_pixel = 7919 * 2 * half % PRIME
    base[0] = modulo(column * per_pixel + channel.astype(F32) * 7919.0)
    base[1] = seed_rows
    base[2] = factor_rows
    base[3] = scale_rows
    real = base.at[4]
    real[...] = jnp.where(item_of < items * SIDE, 1.0, 0.0)

    out_copies = []
    for h, taps in ((0, tap_a), (1, tap_b)):
        x_copies[h].wait()
        staged = fx.at[pl.ds(h * tiles, tiles)]
        gather_rows(maps.at[:, :, pl.ds(h * half, half)], staged, items)
        build_tiled(staged, taps, items, pitch)
        copy = pltpu.make_async_copy(taps.at[1, :, pl.ds(1, SIDE)], x0_out.at[h], o_sem.at[h])
        copy.start()
        out_copies.append(copy)
    b_local.wait()
    b_remote.wait()

    def weights_ready(layer, g):
        @pl.when(section == layer)
        def _():
            w_local[g].wait()

        @pl.when(section != layer)
        def _():
            w_remote[g].wait_recv()

        @pl.loop(0, 3)
        def _(k):
            t = g * 3 + k
            hi, lo = split(wstage[layer, pl.ds(pl.multiple_of(t * 2 * half, 2 * half), 2 * half), :])
            wbf[0, t] = hi
            wbf[1, t] = lo

    def product(parts, first):
        def tile(start, count):
            total = None
            for taps, t, rows in parts:
                row, col = t // 3, t % 3
                for a, b in ((0, 0), (1, 0), (0, 1)):
                    v = taps[col, a, pl.ds(start + row, count)].reshape(count * pitch, half)
                    term = dot(v, wbf[b, t, rows, :])
                    total = term if total is None else total + term
            total = total.reshape(count, pitch, half)
            where = pl.ds(start, count)
            acc[where] = total if first else acc[where] + total

        each_tile(tile)

    for g in range(3):
        weights_ready(0, g)
        product(
            [
                (taps, g * 3 + k, slice(h * half, (h + 1) * half))
                for h, taps in ((0, tap_a), (1, tap_b))
                for k in range(3)
            ],
            g == 0,
        )

    my_half = mine(half)
    bias4 = bias[0, :, my_half]

    @pl.loop(0, SIDE)
    def _(row):
        z = acc[row] + bias4
        acc[row] = z
        fh[0, row, pl.ds(HEAD, pitch)] = z * sigmoid(z) * real[...]

    h_remote = pltpu.make_async_remote_copy(
        fh.at[0, :, pl.ds(HEAD, pitch)], fh.at[1, :, pl.ds(HEAD, pitch)],
        h_sem.at[0], h_sem.at[1], device_id=partner, device_id_type=MESH,
    )
    h_remote.start()
    z4_copy = pltpu.make_async_copy(acc, z4_out, o_sem.at[2])
    z4_copy.start()
    build_taps(fh.at[0], tap_c, items, pitch)
    copy = pltpu.make_async_copy(tap_c.at[1, :, pl.ds(1, SIDE)], h0_out.at[section], o_sem.at[3])
    copy.start()
    out_copies.append(copy)
    for g in range(3):
        weights_ready(1, g)
    z4_copy.wait()
    product([(tap_c, t, my_half) for t in range(9)], True)
    h_remote.wait_recv()
    out_copies[0].wait()
    build_taps(fh.at[1], tap_a, items, pitch)
    copy = pltpu.make_async_copy(tap_a.at[1, :, pl.ds(1, SIDE)], h0_out.at[other], o_sem.at[0])
    copy.start()
    out_copies[0] = copy
    product([(tap_a, t, theirs(half)) for t in range(9)], False)
    bias5 = bias[1, :, my_half]
    for copy in out_copies:
        copy.wait()
    h_remote.wait_send()

    @pl.loop(0, SIDE)
    def _(row):
        z = acc[row] + bias5
        s = sigmoid(z)
        a = z * s
        for tile in range(tiles):
            fx[tile, row, pl.ds(HEAD, pitch)] = a[:, tile * LANES : (tile + 1) * LANES]
        shift = (row * (per_pixel * SIDE)) % PRIME
        a = base[0] + shift.astype(F32)
        a = jnp.where(a >= PRIME, a - PRIME, a)
        hashed = modulo(a * base[2] + base[1])
        cotangent = (hashed / 32760.0 - 1.0) * base[3] * real[...]
        fh[0, row, pl.ds(HEAD, pitch)] = cotangent * (s * (1.0 + z * (1.0 - s)))

    last = [
        pltpu.make_async_copy(fx.at[pl.ds(0, tiles), :, pl.ds(HEAD, pitch)], act_out, o_sem.at[0]),
        pltpu.make_async_copy(fh.at[0, :, pl.ds(HEAD, pitch)], d5_out, o_sem.at[1]),
    ]
    for copy in last:
        copy.start()
    for copy in w_remote:
        copy.wait_send()
    rows_remote.wait()
    for copy in last:
        copy.wait()


def forward(x, weights, biases, seeds, lengths, items, pitch):
    channels = x.shape[2]
    half = channels // 2
    tiles = half // LANES
    maps = (SIDE, pitch, half)
    tiled = jax.ShapeDtypeStruct((tiles, SIDE, pitch, LANES), F32)
    any_spec = pl.BlockSpec(memory_space=pl.ANY)
    smem = pl.BlockSpec(memory_space=pltpu.SMEM)
    taps = pltpu.VMEM((3, 2, SIDE + 2, pitch, half), BF16)
    staged = pltpu.VMEM((2, SIDE, HEAD + pitch + HEAD, half), F32)
    dma = pltpu.SemaphoreType.DMA
    terms = jax.ShapeDtypeStruct((2, 2) + maps, BF16)
    one = jax.ShapeDtypeStruct(maps, F32)
    return pl.pallas_call(
        functools.partial(forward_kernel, items, pitch),
        name="forward",
        out_shape=[tiled, one, one, terms, terms, jax.ShapeDtypeStruct((9, half, channels), F32)],
        in_specs=[smem, smem, any_spec, any_spec, any_spec],
        out_specs=[any_spec] * 6,
        scratch_shapes=[
            pltpu.VMEM(x.shape, F32),
            pltpu.VMEM((2 * tiles, SIDE, HEAD + pitch + HEAD, LANES), F32),
            staged, taps, taps, taps,
            pltpu.VMEM((2, 9 * channels, half), F32),
            pltpu.VMEM((2, 9, channels, half), BF16),
            pltpu.VMEM(maps, F32),
            pltpu.VMEM((2, 1, channels), F32),
            pltpu.VMEM((5, pitch, half), F32),
            dma((2,)), dma((3,)), dma((3,)), dma((3,)), dma((2,)), dma((2,)), dma((3,)), dma((4,)),
        ],
        compiler_params=pltpu.CompilerParams(
            collective_id=0, has_side_effects=True, vmem_limit_bytes=62 * 2**20
        ),
    )(seeds, lengths, x, weights, biases)


WAIT = 3
LAG = 3
RING = 24


def exchange(n, own, r_first, r_line, r_last, fin, gx, wg, sems):
    sent, f_r, z_r, l_r, a_r, c_s, g_r, p_r = sems
    half = own.shape[1]
    part, chunk = half // 2, half // 8
    units = gx.shape[1] // half
    section, dp = lax.axis_index("section"), lax.axis_index("dp")
    x, y, z = lax.rem(dp, 2), lax.rem(lax.div(dp, 2), 2), lax.div(dp, 4)
    kind, slot = lax.rem(n, 2), lax.rem(n, RING)
    later = lax.div(n, units)
    layer, row0 = 1 - later, (n - later * units) * half
    keep = x + kind * (y - x)
    to_x, to_y = dp + 1 - 2 * x, dp + 2 - 4 * y
    first = {"dp": to_x + kind * (to_y - to_x)}
    last = {"dp": to_y + kind * (to_x - to_y)}
    up = {"dp": dp + 4 - 8 * lax.div(z, 3)}
    down = {"dp": dp - 4 + 8 * lax.div(3 - z, 3)}
    base = keep * part

    def rows(start, size):
        return pl.ds(pl.multiple_of(start, chunk), size)

    def remote(src, dst, recv, device):
        return pltpu.make_async_remote_copy(
            src, dst, sent.at[slot], recv, device_id=device, device_id_type=MESH
        )

    def first_copy():
        src = own.at[slot, rows((1 - keep) * part, part)]
        return remote(src, r_first.at[slot], f_r.at[slot], first)

    def line(way, lo, count):
        return remote(
            own.at[slot, rows(base + lo * chunk, count * chunk)],
            r_line.at[slot, way, pl.ds(lo * chunk, count * chunk)],
            z_r.at[slot, way], (up, down)[way],
        )

    def line_add(way, lo, count):
        line(way, lo, count).wait_recv()
        where = rows(base + lo * chunk, count * chunk)
        own[slot, where] += r_line[slot, way, pl.ds(lo * chunk, count * chunk)]

    def last_copy():
        src = own.at[slot, rows(base + z * chunk, chunk)]
        return remote(src, r_last.at[slot], l_r.at[slot], last)

    columns = pl.ds(pl.multiple_of(section * half, half), half)

    def home(body):
        @pl.when(layer == section)
        def _():
            body(lambda start, size: wg.at[rows(row0 + start, size), columns])

        @pl.when(layer != section)
        def _():
            body(lambda start, size: gx.at[layer, rows(row0 + start, size)])

    def spread(where, way, lo, count, src=None):
        dst = where(base + lo * chunk, count * chunk)
        return remote(dst if src is None else src, dst, a_r.at[slot, way], (up, down)[way])

    def keep_copy(where):
        return pltpu.make_async_copy(fin.at[slot], where(base + z * chunk, chunk), c_s.at[slot])

    def back_copy(where):
        kept = where(base, part)
        return remote(kept, kept, g_r.at[slot], first)

    def put_copy():
        unit, target = gx.at[layer, rows(row0, half)], wg.at[rows(row0, half), columns]
        return remote(unit, target, p_r.at[slot], {"section": 1 - section})

    def stage0():
        first_copy().start()

    def stage1():
        first_copy().wait_recv()
        own[slot, rows(base, part)] += r_first[slot]
        pl.when(z == 0)(lambda: line(0, 1, 3).start())
        pl.when(z == 3)(lambda: line(1, 0, 3).start())

    def stage2():
        @pl.when(z == 1)
        def _():
            line_add(0, 1, 3)
            line(0, 2, 2).start()

        @pl.when(z == 2)
        def _():
            line_add(1, 0, 3)
            line(1, 0, 2).start()

    def stage3():
        @pl.when(z == 1)
        def _():
            line_add(1, 0, 2)
            line(1, 0, 1).start()

        @pl.when(z == 2)
        def _():
            line_add(0, 2, 2)
            line(0, 3, 1).start()

    def stage4():
        pl.when(z == 0)(lambda: line_add(1, 0, 1))
        pl.when(z == 3)(lambda: line_add(0, 3, 1))
        last_copy().start()

    def stage5():
        last_copy().wait_recv()
        fin[slot] = own[slot, rows(base + z * chunk, chunk)] + r_last[slot]

        def body(where):
            keep_copy(where).start()
            pl.when(z == 0)(lambda: spread(where, 0, 0, 1, fin.at[slot]).start())
            pl.when(z == 3)(lambda: spread(where, 1, 3, 1, fin.at[slot]).start())

        home(body)

    def stage6():
        def body(where):
            @pl.when(z == 1)
            def _():
                keep_copy(where).wait()
                spread(where, 0, 0, 1).wait_recv()
                spread(where, 0, 0, 2).start()

            @pl.when(z == 2)
            def _():
                keep_copy(where).wait()
                spread(where, 1, 3, 1).wait_recv()
                spread(where, 1, 2, 2).start()

        home(body)

    def stage7():
        def body(where):
            @pl.when(z == 1)
            def _():
                spread(where, 1, 2, 2).wait_recv()
                spread(where, 1, 1, 3).start()

            @pl.when(z == 2)
            def _():
                spread(where, 0, 0, 2).wait_recv()
                spread(where, 0, 0, 3).start()

        home(body)

    def stage8():
        def body(where):
            @pl.when(z == 0)
            def _():
                keep_copy(where).wait()
                spread(where, 1, 1, 3).wait_recv()

            @pl.when(z == 3)
            def _():
                keep_copy(where).wait()
                spread(where, 0, 0, 3).wait_recv()

            back_copy(where).start()

        home(body)

    def stage9():
        home(lambda where: back_copy(where).wait_recv())
        pl.when(layer != section)(lambda: put_copy().start())

    def stage10():
        pl.when(layer == section)(lambda: put_copy().wait_recv())
        inner = (z == 1) | (z == 2)
        for middle, put, count in ((0, 0, 13), (0, 1, 21), (1, 0, 17), (1, 1, 25)):

            @pl.when((inner == (middle == 1)) & ((layer != section) == (put == 1)))
            def _(count=count):
                whole = gx.at[layer, pl.ds(0, count * chunk)]
                remote(whole, whole, p_r.at[slot], {"section": 1 - section}).wait_send()

    return [
        stage0, stage1, stage2, stage3, stage4, stage5, stage6, stage7, stage8, stage9, stage10,
    ]


OFFSETS = (0, 5, 9, 12, 15, 19, 22, 25, 28, 33, 35)


def backward_kernel(
    items, pitch, reduce,
    d5_hbm, z4_hbm, h0_hbm, x0_hbm, w_hbm, wr_hbm,
    gin_out, gx_out, wg_out, bg_out,
    fd, taps, feature, z4, acc, wstage, wbf, own, r_first, r_line, r_last, fin, b_send, b_recv, b_row,
    l_sem, w_sem, d_sem, bs_sem, br_sem, bo_sem, *sems,
):
    section, dp = lax.axis_index("section"), lax.axis_index("dp")
    other = 1 - section
    partner = {"section": other}
    half = acc.shape[2]
    rows_all = SIDE * pitch
    units = 18
    x, y, z = dp % 2, dp // 2 % 2, dp // 4
    pairs = [{"dp": dp + 1 - 2 * x}, {"dp": dp + 2 - 4 * y}]
    pairs += [{"dp": dp + 4 - 8 * (z % 2)}, {"dp": dp + 8 - 16 * (z // 2)}]
    barrier = pltpu.get_barrier_semaphore()

    def greet(device):
        pl.semaphore_signal(barrier, inc=1, device_id=device, device_id_type=MESH)

    greet(partner)
    if reduce:
        for device in pairs:
            greet(device)
        pl.when(z == 1)(lambda: greet({"dp": dp + 4}))
        pl.when(z == 2)(lambda: greet({"dp": dp - 4}))

    def mine(width):
        return pl.ds(pl.multiple_of(section * width, width), width)

    d_local = pltpu.make_async_copy(d5_hbm, fd.at[0, :, pl.ds(HEAD, pitch)], l_sem.at[0])
    h_local = pltpu.make_async_copy(h0_hbm, feature.at[1], l_sem.at[1])
    z_local = pltpu.make_async_copy(z4_hbm, z4, l_sem.at[2])
    x_local = pltpu.make_async_copy(x0_hbm, feature.at[0], l_sem.at[3])
    d_local.start()
    h_local.start()

    def w_copy(q, act):
        layer, slot = 1 - q // 3, q % 2
        three = pl.ds(q % 3 * 3, 3)
        whole = w_hbm.at[0].reshape(9, 2 * half, 2 * half)

        @pl.when(layer == section)
        def _():
            src = whole.at[three, mine(half)]
            act(pltpu.make_async_copy(src, wstage.at[slot], w_sem.at[slot]))

        @pl.when(layer != section)
        def _():
            act(pltpu.make_async_copy(wr_hbm.at[three], wstage.at[slot], w_sem.at[slot]))

    for k in range(3):
        clear_margins(fd.at[k], items, pitch)
    for k in range(2):
        clear_edges(taps.at[k])

    def d_remote(k):
        src = d5_hbm if k == 0 else fd.at[0, :, pl.ds(HEAD, pitch)]
        return pltpu.make_async_remote_copy(
            src, fd.at[1 + k, :, pl.ds(HEAD, pitch)],
            d_sem.at[k, 0], d_sem.at[k, 1], device_id=partner, device_id_type=MESH,
        )

    real = lax.broadcasted_iota(jnp.int32, (pitch, half), 0) < items * SIDE

    def column_sums():
        def add(row, total):
            v = fd[0, row, pl.ds(HEAD, pitch)]
            return total + jnp.sum(v.reshape(pitch // 8, 8, half), axis=0)

        return jnp.sum(lax.fori_loop(0, SIDE, add, jnp.zeros((8, half), F32)), axis=0, keepdims=True)

    d_local.wait()
    build_taps(fd.at[0], taps.at[0], items, pitch)
    pl.semaphore_wait(barrier, 5 + (z + 1) // 2 % 2 if reduce else 1)
    d_remote(0).start()
    w_copy(0, lambda copy: copy.start())
    z_local.start()
    x_local.start()
    b_send[0, 0:8] = jnp.broadcast_to(column_sums(), (8, half))
    acc[...] = jnp.zeros_like(acc)
    h_local.wait()

    def enter(layer):
        z_local.wait()
        x_local.wait()

        @pl.loop(0, SIDE)
        def _(row):
            v = z4[row]
            s = sigmoid(v)
            d = acc[row] * (s * (1.0 + v * (1.0 - s)))
            fd[0, row, pl.ds(HEAD, pitch)] = jnp.where(real, d, 0.0)

        d_remote(1).start()
        build_taps(fd.at[0], taps.at[0], items, pitch)
        which = lax.broadcasted_iota(jnp.int32, (8, half), 0) == 0
        b_send[0] = jnp.where(which, jnp.broadcast_to(column_sums(), (8, half)), b_send[0])
        acc[...] = jnp.zeros_like(acc)

    def receive(k):
        d_remote(k).wait_recv()
        build_taps(fd.at[1 + k], taps.at[1], items, pitch)

    def kernel_unit(n):
        layer, step = 1 - n // units, n % units
        t, m = step // 2, step % 2
        row, col = 2 - t // 3, 2 - t % 3
        v = [feature[layer, m, term].reshape(rows_all, half) for term in range(2)]
        d = [window(taps.at[0], col, term, row) for term in range(2)]
        terms = ((0, 0), (1, 0), (0, 1))
        tail = rows_all % 256
        cut = rows_all - tail if 3 * tail <= 256 else rows_all
        total = None
        for a, b in terms:
            part = dot_tn(v[a][:cut], d[b][:cut])
            total = part if total is None else total + part
        if cut < rows_all:
            total += dot_tn(
                jnp.concatenate([v[a][cut:] for a, b in terms], 0),
                jnp.concatenate([d[b][cut:] for a, b in terms], 0),
            )
        own[n % RING] = total

    def input_piece(layer, p):
        g, j = p // 6, p % 6
        q = 3 * (1 - layer) + g

        @pl.when(j == 0)
        def _():
            w_copy(q, lambda copy: copy.wait())
            pl.when(q + 1 < 6)(lambda: w_copy(q + 1, lambda copy: copy.start()))
            for k in range(3):
                wbf[0, k], wbf[1, k] = split(wstage[q % 2, k])

        def tile(start, count):
            total = None
            for h in range(2):
                for k in range(3):
                    for a, b in ((0, 0), (1, 0), (0, 1)):
                        v = taps[h, 2 - k, a, pl.ds(start + 2 - g, count)]
                        w = wbf[b, k, :, pl.ds(pl.multiple_of((section + h) % 2 * half, half), half)]
                        part = dot_nt(v.reshape(count * pitch, half), w)
                        total = part if total is None else total + part
            acc[pl.ds(start, count)] += total.reshape(count, pitch, half)

        pl.when(j < 5)(lambda: tile(2 * j, 2))
        pl.when(j == 5)(lambda: tile(10, SIDE - 10))

    def bias_copy(k, device):
        return pltpu.make_async_remote_copy(
            b_send.at[k], b_recv.at[k], bs_sem.at[k], br_sem.at[k], device_id=device, device_id_type=MESH
        )

    put_row = pltpu.make_async_copy(b_row, bg_out, bo_sem.at[0])

    def bias_step(k):
        if k > 0 and k < 5:
            bias_copy(k - 1, pairs[k - 1]).wait_recv()
            b_send[k] = b_send[k - 1] + b_recv[k - 1]
        if k < 4:
            bias_copy(k, pairs[k]).start()
        if k == 4:
            bias_copy(4, partner).start()
        if k == 5:
            bias_copy(4, partner).wait_recv()
            for s in range(2):

                @pl.when(section == s)
                def _(s=s):
                    b_row[:, s * half : (s + 1) * half] = b_send[4, s : s + 1]
                    b_row[:, (1 - s) * half : (2 - s) * half] = b_recv[4, s : s + 1]

            put_row.start()

    tiles = half // LANES
    put_acc = [
        pltpu.make_async_copy(
            acc.at[:, :, pl.ds(tile * LANES, LANES)], gin_out.at[tile], l_sem.at[4 + tile]
        )
        for tile in range(tiles)
    ]

    def local_part(n):
        layer, row0 = 1 - n // units, n % units * half
        dst = gx_out.at[layer, pl.ds(pl.multiple_of(row0, half), half)]
        return pltpu.make_async_copy(own.at[n % RING], dst, sems[0].at[n % RING])

    def service(u, odd):
        for k, offset in enumerate(OFFSETS):
            if k == 0 or offset % 2 != odd:
                continue
            valid, n = unit_of(u - offset // 2)

            @pl.when(valid)
            def _():
                stages = exchange(n, own, r_first, r_line, r_last, fin, gx_out, wg_out, sems)
                stages[k]()

    lag = LAG

    def unit_of(u):
        valid = ((u >= 0) & (u < units)) | ((u >= units + lag) & (u < 2 * units + lag))
        return valid, jnp.where(u < units, u, u - lag)

    late0 = units + lag + WAIT
    last = 2 * units + lag + ((OFFSETS[-1] + 1) // 2 if reduce else WAIT)

    @pl.loop(0, last)
    def _(u):
        valid, n = unit_of(u)
        pl.when(u == lag)(lambda: receive(0))
        pl.when(u == units + lag)(lambda: enter(0))
        pl.when(u == late0)(lambda: receive(1))

        @pl.when(valid)
        def _():
            if not reduce:
                pl.when(n >= RING)(lambda: local_part(n - RING).wait())
            kernel_unit(n)
            if reduce:
                exchange(n, own, r_first, r_line, r_last, fin, gx_out, wg_out, sems)[0]()
            else:
                local_part(n).start()

        if reduce:
            service(u, 0)
        early = (u >= lag) & (u < units + lag)
        late = (u >= late0) & (u < late0 + units)

        @pl.when(early | late)
        def _():
            input_piece(jnp.where(early, 1, 0), jnp.where(early, u - lag, u - late0))


        @pl.when(u == late0 + units - 1)
        def _():
            for copy in put_acc:
                copy.start()

        if reduce:
            service(u, 1)
        for k in range(6 if reduce else 0):
            pl.when(u == units + lag + 2 + 2 * k)(lambda k=k: bias_step(k))

    if not reduce:

        @pl.loop(2 * units - RING, 2 * units)
        def _(n):
            local_part(n).wait()

    if reduce:
        for k in range(5):
            bias_copy(k, (pairs + [partner])[k]).wait_send()
        put_row.wait()
    else:
        put_sums = pltpu.make_async_copy(b_send.at[0], bg_out, bo_sem.at[0])
        put_sums.start()
        put_sums.wait()
    for k in range(2):
        d_remote(k).wait_send()
    for copy in put_acc:
        copy.wait()


def backward(d5, z4, h0, x0, weights, rows_other, items, reduce):
    maps = d5.shape
    _, pitch, half = maps
    channels = 2 * half
    any_spec = pl.BlockSpec(memory_space=pl.ANY)
    dma = pltpu.SemaphoreType.DMA
    shape = jax.ShapeDtypeStruct
    ring = RING
    part, chunk = half // 2, half // 8
    return pl.pallas_call(
        functools.partial(backward_kernel, items, pitch, reduce),
        name="backward",
        out_shape=[
            shape((half // LANES, SIDE, pitch, LANES), F32),
            shape((2, 9 * channels, half), F32),
            shape((9 * channels, channels), F32),
            shape((1, channels) if reduce else (8, half), F32),
        ],
        in_specs=[any_spec] * 6,
        out_specs=[any_spec] * 4,
        scratch_shapes=[
            pltpu.VMEM((3, SIDE, HEAD + pitch + HEAD, half), F32),
            pltpu.VMEM((2, 3, 2, SIDE + 2, pitch, half), BF16),
            pltpu.VMEM((2, 2, 2) + maps, BF16),
            pltpu.VMEM(maps, F32),
            pltpu.VMEM(maps, F32),
            pltpu.VMEM((2, 3, half, channels), F32),
            pltpu.VMEM((2, 3, half, channels), BF16),
            pltpu.VMEM((ring, half, half), F32),
            pltpu.VMEM((ring, part, half), F32),
            pltpu.VMEM((ring, 2, part, half), F32),
            pltpu.VMEM((ring, chunk, half), F32),
            pltpu.VMEM((ring, chunk, half), F32),
            pltpu.VMEM((5, 8, half), F32),
            pltpu.VMEM((5, 8, half), F32),
            pltpu.VMEM((1, channels), F32),
            dma((4 + half // LANES,)), dma((2,)), dma((2, 2)), dma((5,)), dma((5,)), dma((1,)),
            dma((ring,)), dma((ring,)), dma((ring, 2)), dma((ring,)), dma((ring, 2)), dma((ring,)),
            dma((ring,)), dma((ring,)),
        ],
        compiler_params=pltpu.CompilerParams(
            collective_id=1, has_side_effects=True, vmem_limit_bytes=62 * 2**20
        ),
    )(d5, z4, h0, x0, weights, rows_other)


def finish_kernel(
    items, rows_in, act_hbm, gin_hbm, wg_hbm, bias_hbm, act_out, gin_out, wg_out, bias_out,
    act_rows, gin_rows, act, gin, wg, bias, i_sem, o_sem,
):
    pieces = wg.shape[0] // rows_in
    count = pieces + 3

    def incoming(k):
        if k < 2:
            src, dst = ((act_hbm, act_rows), (gin_hbm, gin_rows))[k]
        elif k == count - 1:
            src, dst = bias_hbm, bias
        else:
            rows = pl.ds((k - 2) * rows_in, rows_in)
            src, dst = wg_hbm.at[rows], wg.at[rows]
        return pltpu.make_async_copy(src, dst, i_sem.at[k])

    def outgoing(k):
        if k < 2:
            src, dst = ((act, act_out), (gin, gin_out))[k]
        elif k == count - 1:
            src, dst = bias, bias_out
        else:
            rows = pl.ds((k - 2) * rows_in, rows_in)
            src, dst = wg.at[rows], wg_out.at[0, rows]
        return pltpu.make_async_copy(src, dst, o_sem.at[k])

    for k in range(count):
        incoming(k).start()
    for k, (rows, maps) in enumerate(((act_rows, act), (gin_rows, gin))):
        incoming(k).wait()
        for row in range(SIDE):
            for n in range(items):
                for tile in range(rows.shape[0]):
                    maps[
                        n, row * SIDE : (row + 1) * SIDE, tile * LANES : (tile + 1) * LANES
                    ] = rows[tile, row, pl.ds(n, SIDE, stride=items), :]
        outgoing(k).start()
        for j in range(pieces):
            if j % 2 == k:
                incoming(2 + j).wait()
                outgoing(2 + j).start()
    incoming(count - 1).wait()
    outgoing(count - 1).start()
    for k in range(count):
        outgoing(k).wait()


def finish(act, gin, wg, bias, items):
    half = act.shape[0] * LANES
    any_spec = pl.BlockSpec(memory_space=pl.ANY)
    maps = (items, SIDE * SIDE, half)
    pieces = 6
    dma = pltpu.SemaphoreType.DMA
    return pl.pallas_call(
        functools.partial(finish_kernel, items, wg.shape[0] // pieces),
        name="finish",
        out_shape=[
            jax.ShapeDtypeStruct(maps, F32),
            jax.ShapeDtypeStruct(maps, F32),
            jax.ShapeDtypeStruct((1,) + wg.shape, F32),
            jax.ShapeDtypeStruct(bias.shape, F32),
        ],
        in_specs=[any_spec] * 4,
        out_specs=[any_spec] * 4,
        scratch_shapes=[
            pltpu.VMEM(act.shape, F32),
            pltpu.VMEM(act.shape, F32),
            pltpu.VMEM(maps, F32),
            pltpu.VMEM(maps, F32),
            pltpu.VMEM(wg.shape, F32),
            pltpu.VMEM(bias.shape, F32),
            dma((pieces + 3,)),
            dma((pieces + 3,)),
        ],
        compiler_params=pltpu.CompilerParams(vmem_limit_bytes=62 * 2**20),
    )(act, gin, wg, bias)


def per_device(flow_maps, weights, biases, stack_lengths, grad_seeds):
    items = flow_maps.shape[0]
    channels = flow_maps.shape[2]
    half = channels // 2
    pitch = ceil_to(items * SIDE, 16)
    section = lax.axis_index("section")
    act, z4, d5, h0, x0, rows_other = forward(
        flow_maps, weights, biases, grad_seeds, stack_lengths, items, pitch
    )
    fused = lax.axis_size("dp") == 16
    gin, parts, grad, bias = backward(d5, z4, h0, x0, weights, rows_other, items, fused)
    if not fused:
        parts, bias = lax.psum((parts, bias[:2]), "dp")
        given = lax.dynamic_index_in_dim(parts, 1 - section, 0, keepdims=False)
        kept = lax.dynamic_index_in_dim(parts, section, 0, keepdims=False)
        got = lax.ppermute(given, "section", [(0, 1), (1, 0)])
        first, second = jnp.where(section == 0, kept, got), jnp.where(section == 0, got, kept)
        grad = jnp.concatenate([first, second], axis=1)
        both = lax.all_gather(bias, "section", axis=1, tiled=True)
        bias = lax.dynamic_index_in_dim(both, section, 0)
    act, gin, grad, bias = finish(act, gin, grad, bias, items)
    return (act, gin, grad, bias)


def solution(mesh):
    in_specs = (P("dp", None, None), P("section", None, None), P("section", None), P("dp"), P("dp"))
    out_specs = (
        P("dp", None, "section"),
        P("dp", None, "section"),
        P("section", None, None),
        P("section", None),
    )
    return jax.shard_map(
        per_device, mesh=mesh, in_specs=in_specs, out_specs=out_specs, check_vma=False
    )
```

```python
import functools

import jax
import jax.numpy as jnp
from jax import lax
from jax.experimental import pallas as pl
from jax.experimental.pallas import tpu as pltpu
from jax.sharding import PartitionSpec as P

SIDE = 13
PRIME = 65521
F32, BF16 = jnp.float32, jnp.bfloat16
MESH = pl.DeviceIdType.MESH
LANES = 128
HEAD = 16


def ceil_to(value, unit):
    return -(-value // unit) * unit


def split(v):
    hi = v.astype(BF16)
    return hi, (v - hi.astype(F32)).astype(BF16)


BOOST = 32.0


def boost(v):
    hi = v.astype(BF16)
    wide = hi.astype(F32)
    return hi, (wide + (v - wide) * BOOST).astype(BF16)


def dot(a, b):
    return jnp.dot(a, b, preferred_element_type=F32)


def dot_nt(a, b):
    return lax.dot_general(a, b, (((1,), (1,)), ((), ())), preferred_element_type=F32)


def dot_tn(a, b):
    return lax.dot_general(a, b, (((0,), (0,)), ((), ())), preferred_element_type=F32)


def modulo(v):
    quotient = jnp.floor(v * (1.0 / PRIME) - 1e-4)
    rest = v - quotient * PRIME
    return jnp.where(rest >= PRIME, rest - PRIME, rest)


def clear_margins(staged, items, pitch):
    zeros = jnp.zeros((SIDE, HEAD, staged.shape[2]), F32)
    staged[:, 0:HEAD, :] = zeros
    staged[:, HEAD + pitch : HEAD + pitch + HEAD, :] = zeros


def clear_edges(taps):
    zeros = jnp.zeros(taps.shape[:2] + taps.shape[3:], BF16)
    taps[:, :, 0] = zeros
    taps[:, :, SIDE + 1] = zeros


def build_taps(staged, taps, items, pitch, terms=split, low=None):
    @pl.loop(0, SIDE)
    def _(row):
        build_row(staged, taps, row, items, pitch, terms, low)


def build_row(staged, taps, row, items, pitch, terms=split, low=None):
    for col in range(3):
        start = HEAD + (col - 1) * items
        v = staged[row, start : start + pitch, :]
        taps[col, 0, row + 1], taps[col, 1, row + 1] = terms(v)
        if low is not None and col == 1:
            low[row] = split(v)[1]


def gather_rows(maps, staged, items):
    for row in range(SIDE):
        for n in range(items):
            for tile in range(staged.shape[0]):
                staged[tile, row, pl.ds(HEAD + n, SIDE, stride=items), :] = maps[
                    n, row * SIDE : (row + 1) * SIDE, tile * LANES : (tile + 1) * LANES
                ]


def build_tiled(staged, taps, items, pitch, low):
    @pl.loop(0, SIDE)
    def _(row):
        for col in range(3):
            start = HEAD + (col - 1) * items
            for tile in range(staged.shape[0]):
                v = staged[tile, row, start : start + pitch, :]
                lanes = slice(tile * LANES, (tile + 1) * LANES)
                taps[col, 0, row + 1, :, lanes], taps[col, 1, row + 1, :, lanes] = boost(v)
                if col == 1:
                    low[row, :, lanes] = split(v)[1]


def window(taps, col, term, row):
    piece = taps[col, term, pl.ds(row, SIDE)]
    return piece.reshape(piece.shape[0] * piece.shape[1], piece.shape[2])


def each_tile(body, count=4):
    whole = SIDE // count

    @pl.loop(0, whole)
    def _(k):
        body(k * count, count)

    if SIDE % count:
        body(whole * count, SIDE % count)


def sigmoid(z):
    below = 1.0 + jnp.exp(-jnp.maximum(z, -80.0))
    guess = pl.reciprocal(below, approx=True)
    return guess * (2.0 - below * guess)


def forward_kernel(
    items, pitch,
    seeds, lengths, x_hbm, w_hbm, b_hbm,
    act_out, z4_out, d5_out, h0_out, x0_out, wr_out,
    maps, fx, fh, tap_a, tap_b, tap_c, low, wstage, wbf, acc, bias, base,
    x_sem, wl_sem, ws_sem, wr_sem, row_sem, h_sem, b_sem, o_sem,
):
    section = lax.axis_index("section")
    other = 1 - section
    partner = {"section": other}
    half = acc.shape[2]
    taps3 = 3 * 2 * half
    barrier = pltpu.get_barrier_semaphore()
    pl.semaphore_signal(barrier, inc=1, device_id=partner, device_id_type=MESH)

    def mine(width):
        return pl.ds(pl.multiple_of(section * width, width), width)

    def theirs(width):
        return pl.ds(pl.multiple_of(other * width, width), width)

    x_copies = [
        pltpu.make_async_copy(
            x_hbm.at[:, :, pl.ds(h * half, half)], maps.at[:, :, pl.ds(h * half, half)], x_sem.at[h]
        )
        for h in range(2)
    ]
    for copy in x_copies:
        copy.start()
    w_local, w_remote = [], []
    for g in range(3):
        rows = pl.ds(g * taps3, taps3)
        w_local.append(
            pltpu.make_async_copy(
                w_hbm.at[0, rows, mine(half)], wstage.at[section, rows], wl_sem.at[g]
            )
        )
        w_remote.append(
            pltpu.make_async_remote_copy(
                w_hbm.at[0, rows, theirs(half)], wstage.at[section, rows],
                ws_sem.at[g], wr_sem.at[g], device_id=partner, device_id_type=MESH,
            )
        )
    for copy in w_local:
        copy.start()
    b_local = pltpu.make_async_copy(b_hbm, bias.at[section], b_sem.at[0])
    b_local.start()
    pl.semaphore_wait(barrier, 1)
    b_remote = pltpu.make_async_remote_copy(
        b_hbm, bias.at[section], b_sem.at[1], b_sem.at[2], device_id=partner, device_id_type=MESH
    )
    b_remote.start()
    for copy in w_remote:
        copy.start()
    rows_remote = pltpu.make_async_remote_copy(
        w_hbm.at[0].reshape(9, 2 * half, 2 * half).at[:, theirs(half)], wr_out,
        row_sem.at[0], row_sem.at[1], device_id=partner, device_id_type=MESH,
    )
    rows_remote.start()

    for taps in (tap_a, tap_b, tap_c):
        clear_edges(taps)
    tiles = half // LANES
    for tile in range(2 * tiles):
        fx[tile] = jnp.zeros(fx.shape[1:], F32)
    for h in range(2):
        clear_margins(fh.at[h], items, pitch)

    item_of = lax.broadcasted_iota(jnp.int32, (pitch, half), 0)
    column = jnp.floor((item_of.astype(F32) + 0.5) * (1.0 / items))
    item_row = item_of.astype(F32) - column * items
    seed_rows = jnp.zeros((pitch, half), F32)
    factor_rows = jnp.zeros((pitch, half), F32)
    scale_rows = jnp.zeros((pitch, half), F32)
    for n in range(items):
        hit = item_row == float(n)
        seed = seeds[n]
        seed_rows = jnp.where(hit, seed.astype(F32), seed_rows)
        factor_rows = jnp.where(hit, (seed % 251 + 2).astype(F32), factor_rows)
        scale_rows = jnp.where(hit, lengths[n].astype(F32) * 0.1, scale_rows)
    channel = lax.broadcasted_iota(jnp.int32, (pitch, half), 1) + section * half
    per_pixel = 7919 * 2 * half % PRIME
    base[0] = modulo(column * per_pixel + channel.astype(F32) * 7919.0)
    base[1] = seed_rows
    base[2] = factor_rows
    real = base.at[4]
    real[...] = jnp.where(item_of < items * SIDE, 1.0, 0.0)
    base[3] = scale_rows * real[...]

    out_copies = []

    def put_terms(taps, rest, out, k):
        copies = [
            pltpu.make_async_copy(taps.at[1, 0, pl.ds(1, SIDE)], out.at[0], o_sem.at[2 * k]),
            pltpu.make_async_copy(rest, out.at[1], o_sem.at[2 * k + 1]),
        ]
        for copy in copies:
            copy.start()
        return copies

    for h, taps in ((0, tap_a), (1, tap_b)):
        x_copies[h].wait()
        staged = fx.at[pl.ds(h * tiles, tiles)]
        gather_rows(maps.at[:, :, pl.ds(h * half, half)], staged, items)
        build_tiled(staged, taps, items, pitch, low.at[h])
        out_copies += put_terms(taps, low.at[h], x0_out.at[h], h)
    b_local.wait()
    b_remote.wait()

    def weights_ready(layer, g):
        @pl.when(section == layer)
        def _():
            w_local[g].wait()

        @pl.when(section != layer)
        def _():
            w_remote[g].wait_recv()

    def convert(layer, g):
        for k in range(3):
            t = g * 3 + k
            rows = pl.ds(t * 2 * half, 2 * half)
            if not isinstance(t, int):
                rows = pl.ds(pl.multiple_of(t * 2 * half, 2 * half), 2 * half)
            wbf[0, t], wbf[1, t] = boost(wstage[layer, rows, :])

    def product(parts, first):
        def tile(start, count):
            totals = [None, None]
            for taps, t, rows in parts:
                row, col = t // 3, t % 3
                if row == 2 and isinstance(start, int) and start == SIDE - 1:
                    continue
                for a in range(2):
                    v = taps[col, a, pl.ds(start + row, count)].reshape(count * pitch, half)
                    term = dot(v, wbf[a, t, rows, :])
                    totals[a] = term if totals[a] is None else totals[a] + term
            if totals[0] is None:
                return
            total = totals[0] + (totals[1] - totals[0]) * (1.0 / BOOST)
            total = total.reshape(count, pitch, half)
            where = pl.ds(start, count)
            acc[where] = total if first else acc[where] + total

        each_tile(tile)

    my_half = mine(half)
    bias4, bias5 = bias[0, :, my_half], bias[1, :, my_half]

    def hidden(start, count):
        for k in range(count):
            row = start + k
            z = acc[row] + bias4
            acc[row] = z
            fh[0, row, pl.ds(HEAD, pitch)] = z * sigmoid(z) * real[...]
            build_row(fh.at[0], tap_c, row, items, pitch, boost, low.at[2])

    for g in range(3):
        weights_ready(0, g)
        convert(0, g)
        product(
            [
                (taps, g * 3 + k, slice(h * half, (h + 1) * half))
                for h, taps in ((0, tap_a), (1, tap_b))
                for k in range(3)
            ],
            g == 0,
        )

    h_remote = pltpu.make_async_remote_copy(
        fh.at[0, :, pl.ds(HEAD, pitch)], fh.at[1, :, pl.ds(HEAD, pitch)],
        h_sem.at[0], h_sem.at[1], device_id=partner, device_id_type=MESH,
    )
    pl.loop(0, SIDE)(lambda row: hidden(row, 1))
    h_remote.start()
    z4_copy = pltpu.make_async_copy(acc, z4_out, o_sem.at[6])
    z4_copy.start()
    out_copies += put_terms(tap_c, low.at[2], h0_out.at[section], 2)
    for g in range(3):
        weights_ready(1, g)
        convert(1, g)
    z4_copy.wait()
    product([(tap_c, t, my_half) for t in range(9)], True)
    h_remote.wait_recv()
    for copy in out_copies[:2]:
        copy.wait()
    build_taps(fh.at[1], tap_a, items, pitch, boost, low.at[3])
    out_copies = out_copies[2:] + put_terms(tap_a, low.at[3], h0_out.at[other], 0)
    h_remote.wait_send()

    def outputs(start, count):
        for k in range(count):
            row = start + k
            z = acc[row] + bias5
            s = sigmoid(z)
            value = z * s
            for tile in range(tiles):
                fx[tile, row, pl.ds(HEAD, pitch)] = value[:, tile * LANES : (tile + 1) * LANES]
            a = base[0] + row * (per_pixel * SIDE % PRIME) % PRIME * 1.0
            a = jnp.where(a >= PRIME, a - PRIME, a)
            hashed = modulo(a * base[2] + base[1])
            cotangent = (hashed * (1.0 / 32760.0) - 1.0) * base[3]
            fh[0, row, pl.ds(HEAD, pitch)] = cotangent * (s * (1.0 + z * (1.0 - s)))

    product([(tap_a, t, theirs(half)) for t in range(9)], False)
    pl.loop(0, SIDE)(lambda row: outputs(row, 1))
    last = [
        pltpu.make_async_copy(fx.at[pl.ds(0, tiles), :, pl.ds(HEAD, pitch)], act_out, o_sem.at[7]),
        pltpu.make_async_copy(fh.at[0, :, pl.ds(HEAD, pitch)], d5_out, o_sem.at[8]),
    ]
    for copy in last:
        copy.start()
    for copy in w_remote:
        copy.wait_send()
    rows_remote.wait()
    for copy in out_copies + last:
        copy.wait()


def forward(x, weights, biases, seeds, lengths, items, pitch):
    channels = x.shape[2]
    half = channels // 2
    tiles = half // LANES
    maps = (SIDE, pitch, half)
    tiled = jax.ShapeDtypeStruct((tiles, SIDE, pitch, LANES), F32)
    any_spec = pl.BlockSpec(memory_space=pl.ANY)
    smem = pl.BlockSpec(memory_space=pltpu.SMEM)
    taps = pltpu.VMEM((3, 2, SIDE + 2, pitch, half), BF16)
    staged = pltpu.VMEM((2, SIDE, HEAD + pitch + HEAD, half), F32)
    dma = pltpu.SemaphoreType.DMA
    terms = jax.ShapeDtypeStruct((2, 2) + maps, BF16)
    one = jax.ShapeDtypeStruct(maps, F32)
    return pl.pallas_call(
        functools.partial(forward_kernel, items, pitch),
        name="forward",
        out_shape=[tiled, one, one, terms, terms, jax.ShapeDtypeStruct((9, half, channels), F32)],
        in_specs=[smem, smem, any_spec, any_spec, any_spec],
        out_specs=[any_spec] * 6,
        scratch_shapes=[
            pltpu.VMEM(x.shape, F32),
            pltpu.VMEM((2 * tiles, SIDE, HEAD + pitch + HEAD, LANES), F32),
            staged, taps, taps, taps,
            pltpu.VMEM((4,) + maps, BF16),
            pltpu.VMEM((2, 9 * channels, half), F32),
            pltpu.VMEM((2, 9, channels, half), BF16),
            pltpu.VMEM(maps, F32),
            pltpu.VMEM((2, 1, channels), F32),
            pltpu.VMEM((5, pitch, half), F32),
            dma((2,)), dma((3,)), dma((3,)), dma((3,)), dma((2,)), dma((2,)), dma((3,)), dma((9,)),
        ],
        compiler_params=pltpu.CompilerParams(
            collective_id=0, has_side_effects=True, vmem_limit_bytes=62 * 2**20
        ),
    )(seeds, lengths, x, weights, biases)


WAIT = 3
LAG = 3
RING = 24


def exchange(n, own, r_first, r_line, r_last, fin, gx, wg, sems):
    sent, f_r, z_r, l_r, a_r, c_s, g_r, p_r = sems
    half = own.shape[1]
    part, chunk = half // 2, half // 8
    units = gx.shape[1] // half
    section, dp = lax.axis_index("section"), lax.axis_index("dp")
    x, y, z = lax.rem(dp, 2), lax.rem(lax.div(dp, 2), 2), lax.div(dp, 4)
    kind, slot = lax.rem(n, 2), lax.rem(n, RING)
    later = lax.div(n, units)
    layer, row0 = 1 - later, (n - later * units) * half
    keep = x + kind * (y - x)
    to_x, to_y = dp + 1 - 2 * x, dp + 2 - 4 * y
    first = {"dp": to_x + kind * (to_y - to_x)}
    last = {"dp": to_y + kind * (to_x - to_y)}
    up = {"dp": dp + 4 - 8 * lax.div(z, 3)}
    down = {"dp": dp - 4 + 8 * lax.div(3 - z, 3)}
    base = keep * part

    def rows(start, size):
        return pl.ds(pl.multiple_of(start, chunk), size)

    def remote(src, dst, recv, device):
        return pltpu.make_async_remote_copy(
            src, dst, sent.at[slot], recv, device_id=device, device_id_type=MESH
        )

    def first_copy():
        src = own.at[slot, rows((1 - keep) * part, part)]
        return remote(src, r_first.at[slot], f_r.at[slot], first)

    def line(way, lo, count):
        return remote(
            own.at[slot, rows(base + lo * chunk, count * chunk)],
            r_line.at[slot, way, pl.ds(lo * chunk, count * chunk)],
            z_r.at[slot, way], (up, down)[way],
        )

    def line_add(way, lo, count):
        line(way, lo, count).wait_recv()
        where = rows(base + lo * chunk, count * chunk)
        own[slot, where] += r_line[slot, way, pl.ds(lo * chunk, count * chunk)]

    def last_copy():
        src = own.at[slot, rows(base + z * chunk, chunk)]
        return remote(src, r_last.at[slot], l_r.at[slot], last)

    columns = pl.ds(pl.multiple_of(section * half, half), half)

    def home(body):
        @pl.when(layer == section)
        def _():
            body(lambda start, size: wg.at[rows(row0 + start, size), columns])

        @pl.when(layer != section)
        def _():
            body(lambda start, size: gx.at[layer, rows(row0 + start, size)])

    def spread(where, way, lo, count, src=None):
        dst = where(base + lo * chunk, count * chunk)
        return remote(dst if src is None else src, dst, a_r.at[slot, way], (up, down)[way])

    def keep_copy(where):
        return pltpu.make_async_copy(fin.at[slot], where(base + z * chunk, chunk), c_s.at[slot])

    def back_copy(where):
        kept = where(base, part)
        return remote(kept, kept, g_r.at[slot], first)

    def put_copy():
        unit, target = gx.at[layer, rows(row0, half)], wg.at[rows(row0, half), columns]
        return remote(unit, target, p_r.at[slot], {"section": 1 - section})

    def stage0():
        first_copy().start()

    def stage1():
        first_copy().wait_recv()
        own[slot, rows(base, part)] += r_first[slot]
        pl.when(z == 0)(lambda: line(0, 1, 3).start())
        pl.when(z == 3)(lambda: line(1, 0, 3).start())

    def stage2():
        @pl.when(z == 1)
        def _():
            line_add(0, 1, 3)
            line(0, 2, 2).start()

        @pl.when(z == 2)
        def _():
            line_add(1, 0, 3)
            line(1, 0, 2).start()

    def stage3():
        @pl.when(z == 1)
        def _():
            line_add(1, 0, 2)
            line(1, 0, 1).start()

        @pl.when(z == 2)
        def _():
            line_add(0, 2, 2)
            line(0, 3, 1).start()

    def stage4():
        pl.when(z == 0)(lambda: line_add(1, 0, 1))
        pl.when(z == 3)(lambda: line_add(0, 3, 1))
        last_copy().start()

    def stage5():
        last_copy().wait_recv()
        fin[slot] = own[slot, rows(base + z * chunk, chunk)] + r_last[slot]

        def body(where):
            keep_copy(where).start()
            pl.when(z == 0)(lambda: spread(where, 0, 0, 1, fin.at[slot]).start())
            pl.when(z == 3)(lambda: spread(where, 1, 3, 1, fin.at[slot]).start())

        home(body)

    def stage6():
        def body(where):
            @pl.when(z == 1)
            def _():
                keep_copy(where).wait()
                spread(where, 0, 0, 1).wait_recv()
                spread(where, 0, 0, 2).start()

            @pl.when(z == 2)
            def _():
                keep_copy(where).wait()
                spread(where, 1, 3, 1).wait_recv()
                spread(where, 1, 2, 2).start()

        home(body)

    def stage7():
        def body(where):
            @pl.when(z == 1)
            def _():
                spread(where, 1, 2, 2).wait_recv()
                spread(where, 1, 1, 3).start()

            @pl.when(z == 2)
            def _():
                spread(where, 0, 0, 2).wait_recv()
                spread(where, 0, 0, 3).start()

        home(body)

    def stage8():
        def body(where):
            @pl.when(z == 0)
            def _():
                keep_copy(where).wait()
                spread(where, 1, 1, 3).wait_recv()

            @pl.when(z == 3)
            def _():
                keep_copy(where).wait()
                spread(where, 0, 0, 3).wait_recv()

            back_copy(where).start()

        home(body)

    def stage9():
        home(lambda where: back_copy(where).wait_recv())
        pl.when(layer != section)(lambda: put_copy().start())

    def stage10():
        pl.when(layer == section)(lambda: put_copy().wait_recv())
        inner = (z == 1) | (z == 2)
        for middle, put, count in ((0, 0, 13), (0, 1, 21), (1, 0, 17), (1, 1, 25)):

            @pl.when((inner == (middle == 1)) & ((layer != section) == (put == 1)))
            def _(count=count):
                whole = gx.at[layer, pl.ds(0, count * chunk)]
                remote(whole, whole, p_r.at[slot], {"section": 1 - section}).wait_send()

    return [
        stage0, stage1, stage2, stage3, stage4, stage5, stage6, stage7, stage8, stage9, stage10,
    ]


OFFSETS = (0, 5, 9, 12, 15, 19, 22, 25, 28, 33, 35)


def backward_kernel(
    items, pitch, reduce,
    d5_hbm, z4_hbm, h0_hbm, x0_hbm, w_hbm, wr_hbm,
    gin_out, gx_out, wg_out, bg_out,
    fd, taps, feature, z4, acc, wstage, wbf, own, r_first, r_line, r_last, fin, b_send, b_recv, b_row,
    l_sem, w_sem, d_sem, bs_sem, br_sem, bo_sem, *sems,
):
    section, dp = lax.axis_index("section"), lax.axis_index("dp")
    other = 1 - section
    partner = {"section": other}
    half = acc.shape[2]
    units = 18
    x, y, z = dp % 2, dp // 2 % 2, dp // 4
    pairs = [{"dp": dp + 1 - 2 * x}, {"dp": dp + 2 - 4 * y}]
    pairs += [{"dp": dp + 4 - 8 * (z % 2)}, {"dp": dp + 8 - 16 * (z // 2)}]
    barrier = pltpu.get_barrier_semaphore()

    def greet(device):
        pl.semaphore_signal(barrier, inc=1, device_id=device, device_id_type=MESH)

    greet(partner)
    if reduce:
        for device in pairs:
            greet(device)
        pl.when(z == 1)(lambda: greet({"dp": dp + 4}))
        pl.when(z == 2)(lambda: greet({"dp": dp - 4}))

    def mine(width):
        return pl.ds(pl.multiple_of(section * width, width), width)

    d_local = pltpu.make_async_copy(d5_hbm, fd.at[0, :, pl.ds(HEAD, pitch)], l_sem.at[0])
    h_local = pltpu.make_async_copy(h0_hbm, feature.at[1], l_sem.at[1])
    z_local = pltpu.make_async_copy(z4_hbm, z4, l_sem.at[2])
    x_local = pltpu.make_async_copy(x0_hbm, feature.at[0], l_sem.at[3])
    d_local.start()
    h_local.start()

    def w_copy(q, act):
        layer, slot = 1 - q // 3, q % 2
        three = pl.ds(q % 3 * 3, 3)
        whole = w_hbm.at[0].reshape(9, 2 * half, 2 * half)

        @pl.when(layer == section)
        def _():
            src = whole.at[three, mine(half)]
            act(pltpu.make_async_copy(src, wstage.at[slot], w_sem.at[slot]))

        @pl.when(layer != section)
        def _():
            act(pltpu.make_async_copy(wr_hbm.at[three], wstage.at[slot], w_sem.at[slot]))

    for k in range(3):
        clear_margins(fd.at[k], items, pitch)
    for k in range(2):
        clear_edges(taps.at[k])

    def d_remote(k):
        src = d5_hbm if k == 0 else fd.at[0, :, pl.ds(HEAD, pitch)]
        return pltpu.make_async_remote_copy(
            src, fd.at[1 + k, :, pl.ds(HEAD, pitch)],
            d_sem.at[k, 0], d_sem.at[k, 1], device_id=partner, device_id_type=MESH,
        )

    real = lax.broadcasted_iota(jnp.int32, (pitch, half), 0) < items * SIDE

    def column_sums():
        def add(row, total):
            v = fd[0, row, pl.ds(HEAD, pitch)]
            return total + jnp.sum(v.reshape(pitch // 8, 8, half), axis=0)

        return jnp.sum(lax.fori_loop(0, SIDE, add, jnp.zeros((8, half), F32)), axis=0, keepdims=True)

    d_local.wait()
    build_taps(fd.at[0], taps.at[0], items, pitch)
    pl.semaphore_wait(barrier, 5 + (z + 1) // 2 % 2 if reduce else 1)
    d_remote(0).start()
    w_copy(0, lambda copy: copy.start())
    z_local.start()
    x_local.start()
    b_send[0, 0:8] = jnp.broadcast_to(column_sums(), (8, half))
    acc[...] = jnp.zeros_like(acc)
    h_local.wait()

    def enter(layer):
        z_local.wait()
        x_local.wait()

        @pl.loop(0, SIDE)
        def _(row):
            v = z4[row]
            s = sigmoid(v)
            d = acc[row] * (s * (1.0 + v * (1.0 - s)))
            fd[0, row, pl.ds(HEAD, pitch)] = jnp.where(real, d, 0.0)

        d_remote(1).start()
        build_taps(fd.at[0], taps.at[0], items, pitch)
        which = lax.broadcasted_iota(jnp.int32, (8, half), 0) == 0
        b_send[0] = jnp.where(which, jnp.broadcast_to(column_sums(), (8, half)), b_send[0])
        acc[...] = jnp.zeros_like(acc)

    def receive(k):
        d_remote(k).wait_recv()
        build_taps(fd.at[1 + k], taps.at[1], items, pitch)

    def kernel_unit(n):
        layer, step = 1 - n // units, n % units
        t, m = step // 2, step % 2
        row, col = 2 - t // 3, 2 - t % 3
        terms = ((0, 0), (1, 0), (0, 1))

        def contract(first, count):
            size = count * pitch
            v = [
                feature[layer, m, term, pl.ds(first, count)].reshape(size, half) for term in range(2)
            ]
            d = [
                taps[0, col, term, pl.ds(first + row, count)].reshape(size, half) for term in range(2)
            ]
            tail = size % 256
            cut = size - tail
            total = None
            for a, b in terms:
                part = dot_tn(v[a][:cut], d[b][:cut])
                total = part if total is None else total + part
            if tail:
                total += dot_tn(
                    jnp.concatenate([v[a][cut:] for a, b in terms], 0),
                    jnp.concatenate([d[b][cut:] for a, b in terms], 0),
                )
            own[n % RING] = total

        pl.when(row == 1)(lambda: contract(0, SIDE))
        pl.when(row != 1)(lambda: contract(jnp.where(row == 0, 1, 0), SIDE - 1))

    def input_piece(layer, p):
        g, j = p // 6, p % 6
        q = 3 * (1 - layer) + g

        @pl.when(j == 0)
        def _():
            w_copy(q, lambda copy: copy.wait())
            pl.when(q + 1 < 6)(lambda: w_copy(q + 1, lambda copy: copy.start()))
            for k in range(3):
                wbf[0, k], wbf[1, k] = split(wstage[q % 2, k])

        def tile(start, count):
            total = None
            for h in range(2):
                for k in range(3):
                    for a, b in ((0, 0), (1, 0), (0, 1)):
                        v = taps[h, 2 - k, a, pl.ds(start + 2 - g, count)]
                        w = wbf[b, k, :, pl.ds(pl.multiple_of((section + h) % 2 * half, half), half)]
                        part = dot_nt(v.reshape(count * pitch, half), w)
                        total = part if total is None else total + part
            acc[pl.ds(start, count)] += total.reshape(count, pitch, half)

        top, bottom = (j == 0) & (g == 2), (j == 5) & (g == 0)
        pl.when((j < 5) & jnp.logical_not(top))(lambda: tile(2 * j, 2))
        pl.when(top)(lambda: tile(1, 1))
        pl.when((j == 5) & (g != 0))(lambda: tile(10, SIDE - 10))
        pl.when(bottom)(lambda: tile(10, SIDE - 11))

    def bias_copy(k, device):
        return pltpu.make_async_remote_copy(
            b_send.at[k], b_recv.at[k], bs_sem.at[k], br_sem.at[k], device_id=device, device_id_type=MESH
        )

    put_row = pltpu.make_async_copy(b_row, bg_out, bo_sem.at[0])

    def bias_step(k):
        if k > 0 and k < 5:
            bias_copy(k - 1, pairs[k - 1]).wait_recv()
            b_send[k] = b_send[k - 1] + b_recv[k - 1]
        if k < 4:
            bias_copy(k, pairs[k]).start()
        if k == 4:
            bias_copy(4, partner).start()
        if k == 5:
            bias_copy(4, partner).wait_recv()
            for s in range(2):

                @pl.when(section == s)
                def _(s=s):
                    b_row[:, s * half : (s + 1) * half] = b_send[4, s : s + 1]
                    b_row[:, (1 - s) * half : (2 - s) * half] = b_recv[4, s : s + 1]

            put_row.start()

    tiles = half // LANES
    put_acc = [
        pltpu.make_async_copy(
            acc.at[:, :, pl.ds(tile * LANES, LANES)], gin_out.at[tile], l_sem.at[4 + tile]
        )
        for tile in range(tiles)
    ]

    def local_part(n):
        layer, row0 = 1 - n // units, n % units * half
        dst = gx_out.at[layer, pl.ds(pl.multiple_of(row0, half), half)]
        return pltpu.make_async_copy(own.at[n % RING], dst, sems[0].at[n % RING])

    def service(u, odd):
        for k, offset in enumerate(OFFSETS):
            if k == 0 or offset % 2 != odd:
                continue
            valid, n = unit_of(u - offset // 2)

            @pl.when(valid)
            def _():
                stages = exchange(n, own, r_first, r_line, r_last, fin, gx_out, wg_out, sems)
                stages[k]()

    lag = LAG

    def unit_of(u):
        valid = ((u >= 0) & (u < units)) | ((u >= units + lag) & (u < 2 * units + lag))
        return valid, jnp.where(u < units, u, u - lag)

    late0 = units + lag + WAIT
    last = 2 * units + lag + ((OFFSETS[-1] + 1) // 2 if reduce else WAIT)

    @pl.loop(0, last)
    def _(u):
        valid, n = unit_of(u)
        pl.when(u == lag)(lambda: receive(0))
        pl.when(u == units + lag)(lambda: enter(0))
        pl.when(u == late0)(lambda: receive(1))

        @pl.when(valid)
        def _():
            if not reduce:
                pl.when(n >= RING)(lambda: local_part(n - RING).wait())
            kernel_unit(n)
            if reduce:
                exchange(n, own, r_first, r_line, r_last, fin, gx_out, wg_out, sems)[0]()
            else:
                local_part(n).start()

        if reduce:
            service(u, 0)
        early = (u >= lag) & (u < units + lag)
        late = (u >= late0) & (u < late0 + units)

        @pl.when(early | late)
        def _():
            input_piece(jnp.where(early, 1, 0), jnp.where(early, u - lag, u - late0))


        @pl.when(u == late0 + units - 1)
        def _():
            for copy in put_acc:
                copy.start()

        if reduce:
            service(u, 1)
        for k in range(6 if reduce else 0):
            pl.when(u == units + lag + 2 + 2 * k)(lambda k=k: bias_step(k))

    if not reduce:

        @pl.loop(2 * units - RING, 2 * units)
        def _(n):
            local_part(n).wait()

    if reduce:
        for k in range(5):
            bias_copy(k, (pairs + [partner])[k]).wait_send()
        put_row.wait()
    else:
        put_sums = pltpu.make_async_copy(b_send.at[0], bg_out, bo_sem.at[0])
        put_sums.start()
        put_sums.wait()
    for k in range(2):
        d_remote(k).wait_send()
    for copy in put_acc:
        copy.wait()


def backward(d5, z4, h0, x0, weights, rows_other, items, reduce):
    maps = d5.shape
    _, pitch, half = maps
    channels = 2 * half
    any_spec = pl.BlockSpec(memory_space=pl.ANY)
    dma = pltpu.SemaphoreType.DMA
    shape = jax.ShapeDtypeStruct
    ring = RING
    part, chunk = half // 2, half // 8
    return pl.pallas_call(
        functools.partial(backward_kernel, items, pitch, reduce),
        name="backward",
        out_shape=[
            shape((half // LANES, SIDE, pitch, LANES), F32),
            shape((2, 9 * channels, half), F32),
            shape((9 * channels, channels), F32),
            shape((1, channels) if reduce else (8, half), F32),
        ],
        in_specs=[any_spec] * 6,
        out_specs=[any_spec] * 4,
        scratch_shapes=[
            pltpu.VMEM((3, SIDE, HEAD + pitch + HEAD, half), F32),
            pltpu.VMEM((2, 3, 2, SIDE + 2, pitch, half), BF16),
            pltpu.VMEM((2, 2, 2) + maps, BF16),
            pltpu.VMEM(maps, F32),
            pltpu.VMEM(maps, F32),
            pltpu.VMEM((2, 3, half, channels), F32),
            pltpu.VMEM((2, 3, half, channels), BF16),
            pltpu.VMEM((ring, half, half), F32),
            pltpu.VMEM((ring, part, half), F32),
            pltpu.VMEM((ring, 2, part, half), F32),
            pltpu.VMEM((ring, chunk, half), F32),
            pltpu.VMEM((ring, chunk, half), F32),
            pltpu.VMEM((5, 8, half), F32),
            pltpu.VMEM((5, 8, half), F32),
            pltpu.VMEM((1, channels), F32),
            dma((4 + half // LANES,)), dma((2,)), dma((2, 2)), dma((5,)), dma((5,)), dma((1,)),
            dma((ring,)), dma((ring,)), dma((ring, 2)), dma((ring,)), dma((ring, 2)), dma((ring,)),
            dma((ring,)), dma((ring,)),
        ],
        compiler_params=pltpu.CompilerParams(
            collective_id=1, has_side_effects=True, vmem_limit_bytes=62 * 2**20
        ),
    )(d5, z4, h0, x0, weights, rows_other)


def finish_kernel(
    items, rows_in, act_hbm, gin_hbm, wg_hbm, bias_hbm, act_out, gin_out, wg_out, bias_out,
    act_rows, gin_rows, act, gin, wg, bias, i_sem, o_sem,
):
    pieces = wg.shape[0] // rows_in
    count = pieces + 3

    def incoming(k):
        if k < 2:
            src, dst = ((act_hbm, act_rows), (gin_hbm, gin_rows))[k]
        elif k == count - 1:
            src, dst = bias_hbm, bias
        else:
            rows = pl.ds((k - 2) * rows_in, rows_in)
            src, dst = wg_hbm.at[rows], wg.at[rows]
        return pltpu.make_async_copy(src, dst, i_sem.at[k])

    def outgoing(k):
        if k < 2:
            src, dst = ((act, act_out), (gin, gin_out))[k]
        elif k == count - 1:
            src, dst = bias, bias_out
        else:
            rows = pl.ds((k - 2) * rows_in, rows_in)
            src, dst = wg.at[rows], wg_out.at[0, rows]
        return pltpu.make_async_copy(src, dst, o_sem.at[k])

    for k in range(count):
        incoming(k).start()
    for k, (rows, maps) in enumerate(((act_rows, act), (gin_rows, gin))):
        incoming(k).wait()
        for row in range(SIDE):
            for n in range(items):
                for tile in range(rows.shape[0]):
                    maps[
                        n, row * SIDE : (row + 1) * SIDE, tile * LANES : (tile + 1) * LANES
                    ] = rows[tile, row, pl.ds(n, SIDE, stride=items), :]
        outgoing(k).start()
        for j in range(pieces):
            if j % 2 == k:
                incoming(2 + j).wait()
                outgoing(2 + j).start()
    incoming(count - 1).wait()
    outgoing(count - 1).start()
    for k in range(count):
        outgoing(k).wait()


def finish(act, gin, wg, bias, items):
    half = act.shape[0] * LANES
    any_spec = pl.BlockSpec(memory_space=pl.ANY)
    maps = (items, SIDE * SIDE, half)
    pieces = 6
    dma = pltpu.SemaphoreType.DMA
    return pl.pallas_call(
        functools.partial(finish_kernel, items, wg.shape[0] // pieces),
        name="finish",
        out_shape=[
            jax.ShapeDtypeStruct(maps, F32),
            jax.ShapeDtypeStruct(maps, F32),
            jax.ShapeDtypeStruct((1,) + wg.shape, F32),
            jax.ShapeDtypeStruct(bias.shape, F32),
        ],
        in_specs=[any_spec] * 4,
        out_specs=[any_spec] * 4,
        scratch_shapes=[
            pltpu.VMEM(act.shape, F32),
            pltpu.VMEM(act.shape, F32),
            pltpu.VMEM(maps, F32),
            pltpu.VMEM(maps, F32),
            pltpu.VMEM(wg.shape, F32),
            pltpu.VMEM(bias.shape, F32),
            dma((pieces + 3,)),
            dma((pieces + 3,)),
        ],
        compiler_params=pltpu.CompilerParams(vmem_limit_bytes=62 * 2**20),
    )(act, gin, wg, bias)


def per_device(flow_maps, weights, biases, stack_lengths, grad_seeds):
    items = flow_maps.shape[0]
    channels = flow_maps.shape[2]
    half = channels // 2
    pitch = ceil_to(items * SIDE, 16)
    section = lax.axis_index("section")
    act, z4, d5, h0, x0, rows_other = forward(
        flow_maps, weights, biases, grad_seeds, stack_lengths, items, pitch
    )
    fused = lax.axis_size("dp") == 16
    gin, parts, grad, bias = backward(d5, z4, h0, x0, weights, rows_other, items, fused)
    if not fused:
        parts, bias = lax.psum((parts, bias[:2]), "dp")
        given = lax.dynamic_index_in_dim(parts, 1 - section, 0, keepdims=False)
        kept = lax.dynamic_index_in_dim(parts, section, 0, keepdims=False)
        got = lax.ppermute(given, "section", [(0, 1), (1, 0)])
        first, second = jnp.where(section == 0, kept, got), jnp.where(section == 0, got, kept)
        grad = jnp.concatenate([first, second], axis=1)
        both = lax.all_gather(bias, "section", axis=1, tiled=True)
        bias = lax.dynamic_index_in_dim(both, section, 0)
    act, gin, grad, bias = finish(act, gin, grad, bias, items)
    return (act, gin, grad, bias)


def solution(mesh):
    in_specs = (P("dp", None, None), P("section", None, None), P("section", None), P("dp"), P("dp"))
    out_specs = (
        P("dp", None, "section"),
        P("dp", None, "section"),
        P("section", None, None),
        P("section", None),
    )
    return jax.shard_map(
        per_device, mesh=mesh, in_specs=in_specs, out_specs=out_specs, check_vma=False
    )
```

```python
import functools

import jax
import jax.numpy as jnp
from jax import lax
from jax.experimental import pallas as pl
from jax.experimental.pallas import tpu as pltpu
from jax.sharding import PartitionSpec as P

SIDE = 13
PRIME = 65521
F32, BF16 = jnp.float32, jnp.bfloat16
MESH = pl.DeviceIdType.MESH
LANES = 128
PARTS = ((0, 5), (5, 9), (9, SIDE))
HEAD = 16


def ceil_to(value, unit):
    return -(-value // unit) * unit


def split(v):
    hi = v.astype(BF16)
    return hi, (v - hi.astype(F32)).astype(BF16)


BOOST = 32.0


def boost(v):
    hi = v.astype(BF16)
    wide = hi.astype(F32)
    return hi, (wide + (v - wide) * BOOST).astype(BF16)


def dot(a, b):
    return jnp.dot(a, b, preferred_element_type=F32)


def dot_nt(a, b):
    return lax.dot_general(a, b, (((1,), (1,)), ((), ())), preferred_element_type=F32)


def dot_tn(a, b):
    return lax.dot_general(a, b, (((0,), (0,)), ((), ())), preferred_element_type=F32)


def modulo(v):
    quotient = jnp.floor(v * (1.0 / PRIME) - 1e-4)
    rest = v - quotient * PRIME
    return jnp.where(rest >= PRIME, rest - PRIME, rest)


def clear_margins(staged, items, pitch):
    zeros = jnp.zeros((SIDE, HEAD, staged.shape[2]), F32)
    staged[:, 0:HEAD, :] = zeros
    staged[:, HEAD + pitch : HEAD + pitch + HEAD, :] = zeros


def clear_edges(taps):
    zeros = jnp.zeros(taps.shape[:2] + taps.shape[3:], BF16)
    taps[:, :, 0] = zeros
    taps[:, :, SIDE + 1] = zeros


def build_taps(staged, taps, items, pitch, terms=split, low=None, span=(0, SIDE)):
    @pl.loop(*span)
    def _(row):
        build_row(staged, taps, row, items, pitch, terms, low)


def build_row(staged, taps, row, items, pitch, terms=split, low=None):
    for col in range(3):
        start = HEAD + (col - 1) * items
        v = staged[row, start : start + pitch, :]
        taps[col, 0, row + 1], taps[col, 1, row + 1] = terms(v)
        if low is not None and col == 1:
            low[row] = split(v)[1]


def gather_rows(maps, staged, items):
    for row in range(SIDE):
        for n in range(items):
            for tile in range(staged.shape[0]):
                staged[tile, row, pl.ds(HEAD + n, SIDE, stride=items), :] = maps[
                    n, row * SIDE : (row + 1) * SIDE, tile * LANES : (tile + 1) * LANES
                ]


def build_tiled(staged, taps, items, pitch, low):
    @pl.loop(0, SIDE)
    def _(row):
        for col in range(3):
            start = HEAD + (col - 1) * items
            for tile in range(staged.shape[0]):
                v = staged[tile, row, start : start + pitch, :]
                lanes = slice(tile * LANES, (tile + 1) * LANES)
                taps[col, 0, row + 1, :, lanes], taps[col, 1, row + 1, :, lanes] = boost(v)
                if col == 1:
                    low[row, :, lanes] = split(v)[1]


def window(taps, col, term, row):
    piece = taps[col, term, pl.ds(row, SIDE)]
    return piece.reshape(piece.shape[0] * piece.shape[1], piece.shape[2])


def each_tile(body, count=4):
    whole = SIDE // count

    @pl.loop(0, whole)
    def _(k):
        body(k * count, count)

    if SIDE % count:
        body(whole * count, SIDE % count)


def sigmoid(z):
    below = 1.0 + jnp.exp(-jnp.maximum(z, -80.0))
    guess = pl.reciprocal(below, approx=True)
    return guess * (2.0 - below * guess)


def forward_kernel(
    items, pitch,
    seeds, lengths, x_hbm, w_hbm, b_hbm,
    act_out, z4_out, d5_out, h0_out, x0_out, wr_out,
    maps, fx, fh, tap_a, tap_b, tap_c, low, wstage, wbf, acc, bias, base,
    x_sem, wl_sem, ws_sem, wr_sem, row_sem, h_sem, b_sem, o_sem,
):
    section = lax.axis_index("section")
    other = 1 - section
    partner = {"section": other}
    half = acc.shape[2]
    taps3 = 3 * 2 * half
    barrier = pltpu.get_barrier_semaphore()
    pl.semaphore_signal(barrier, inc=1, device_id=partner, device_id_type=MESH)

    def mine(width):
        return pl.ds(pl.multiple_of(section * width, width), width)

    def theirs(width):
        return pl.ds(pl.multiple_of(other * width, width), width)

    x_copies = [
        pltpu.make_async_copy(
            x_hbm.at[:, :, pl.ds(h * half, half)], maps.at[:, :, pl.ds(h * half, half)], x_sem.at[h]
        )
        for h in range(2)
    ]
    for copy in x_copies:
        copy.start()
    w_local, w_remote = [], []
    for g in range(3):
        rows = pl.ds(g * taps3, taps3)
        w_local.append(
            pltpu.make_async_copy(
                w_hbm.at[0, rows, mine(half)], wstage.at[section, rows], wl_sem.at[g]
            )
        )
        w_remote.append(
            pltpu.make_async_remote_copy(
                w_hbm.at[0, rows, theirs(half)], wstage.at[section, rows],
                ws_sem.at[g], wr_sem.at[g], device_id=partner, device_id_type=MESH,
            )
        )
    for copy in w_local:
        copy.start()
    b_local = pltpu.make_async_copy(b_hbm, bias.at[section], b_sem.at[0])
    b_local.start()
    pl.semaphore_wait(barrier, 1)
    b_remote = pltpu.make_async_remote_copy(
        b_hbm, bias.at[section], b_sem.at[1], b_sem.at[2], device_id=partner, device_id_type=MESH
    )
    b_remote.start()
    for copy in w_remote:
        copy.start()
    rows_remote = pltpu.make_async_remote_copy(
        w_hbm.at[0].reshape(9, 2 * half, 2 * half).at[:, theirs(half)], wr_out,
        row_sem.at[0], row_sem.at[1], device_id=partner, device_id_type=MESH,
    )
    rows_remote.start()

    for taps in (tap_a, tap_b, tap_c):
        clear_edges(taps)
    tiles = half // LANES
    for tile in range(2 * tiles):
        fx[tile] = jnp.zeros(fx.shape[1:], F32)
    for h in range(2):
        clear_margins(fh.at[h], items, pitch)

    item_of = lax.broadcasted_iota(jnp.int32, (pitch, half), 0)
    column = jnp.floor((item_of.astype(F32) + 0.5) * (1.0 / items))
    item_row = item_of.astype(F32) - column * items
    seed_rows = jnp.zeros((pitch, half), F32)
    factor_rows = jnp.zeros((pitch, half), F32)
    scale_rows = jnp.zeros((pitch, half), F32)
    for n in range(items):
        hit = item_row == float(n)
        seed = seeds[n]
        seed_rows = jnp.where(hit, seed.astype(F32), seed_rows)
        factor_rows = jnp.where(hit, (seed % 251 + 2).astype(F32), factor_rows)
        scale_rows = jnp.where(hit, lengths[n].astype(F32) * 0.1, scale_rows)
    channel = lax.broadcasted_iota(jnp.int32, (pitch, half), 1) + section * half
    per_pixel = 7919 * 2 * half % PRIME
    base[0] = modulo(column * per_pixel + channel.astype(F32) * 7919.0)
    base[1] = seed_rows
    base[2] = factor_rows
    real = base.at[4]
    real[...] = jnp.where(item_of < items * SIDE, 1.0, 0.0)
    base[3] = scale_rows * real[...]

    out_copies = []

    def put_terms(taps, rest, out, k):
        copies = [
            pltpu.make_async_copy(taps.at[1, 0, pl.ds(1, SIDE)], out.at[0], o_sem.at[2 * k]),
            pltpu.make_async_copy(rest, out.at[1], o_sem.at[2 * k + 1]),
        ]
        for copy in copies:
            copy.start()
        return copies

    for h, taps in ((0, tap_a), (1, tap_b)):
        x_copies[h].wait()
        staged = fx.at[pl.ds(h * tiles, tiles)]
        gather_rows(maps.at[:, :, pl.ds(h * half, half)], staged, items)
        build_tiled(staged, taps, items, pitch, low.at[h])
        out_copies += put_terms(taps, low.at[h], x0_out.at[h], h)
    b_local.wait()
    b_remote.wait()

    def weights_ready(layer, g):
        @pl.when(section == layer)
        def _():
            w_local[g].wait()

        @pl.when(section != layer)
        def _():
            w_remote[g].wait_recv()

    def convert(layer, g):
        for k in range(3):
            t = g * 3 + k
            rows = pl.ds(t * 2 * half, 2 * half)
            if not isinstance(t, int):
                rows = pl.ds(pl.multiple_of(t * 2 * half, 2 * half), 2 * half)
            wbf[0, t], wbf[1, t] = boost(wstage[layer, rows, :])

    def product(parts, first):
        def tile(start, count):
            totals = [None, None]
            for taps, t, rows in parts:
                row, col = t // 3, t % 3
                if row == 2 and isinstance(start, int) and start == SIDE - 1:
                    continue
                for a in range(2):
                    v = taps[col, a, pl.ds(start + row, count)].reshape(count * pitch, half)
                    term = dot(v, wbf[a, t, rows, :])
                    totals[a] = term if totals[a] is None else totals[a] + term
            if totals[0] is None:
                return
            total = totals[0] + (totals[1] - totals[0]) * (1.0 / BOOST)
            total = total.reshape(count, pitch, half)
            where = pl.ds(start, count)
            acc[where] = total if first else acc[where] + total

        each_tile(tile)

    my_half = mine(half)
    bias4, bias5 = bias[0, :, my_half], bias[1, :, my_half]

    def hidden(start, count):
        for k in range(count):
            row = start + k
            z = acc[row] + bias4
            acc[row] = z
            fh[0, row, pl.ds(HEAD, pitch)] = z * sigmoid(z) * real[...]
            build_row(fh.at[0], tap_c, row, items, pitch, boost, low.at[2])

    for g in range(3):
        weights_ready(0, g)
        convert(0, g)
        product(
            [
                (taps, g * 3 + k, slice(h * half, (h + 1) * half))
                for h, taps in ((0, tap_a), (1, tap_b))
                for k in range(3)
            ],
            g == 0,
        )

    h_remote = pltpu.make_async_remote_copy(
        fh.at[0, :, pl.ds(HEAD, pitch)], fh.at[1, :, pl.ds(HEAD, pitch)],
        h_sem.at[0], h_sem.at[1], device_id=partner, device_id_type=MESH,
    )
    pl.loop(0, SIDE)(lambda row: hidden(row, 1))
    h_remote.start()
    z4_copy = pltpu.make_async_copy(acc, z4_out, o_sem.at[6])
    z4_copy.start()
    out_copies += put_terms(tap_c, low.at[2], h0_out.at[section], 2)
    for g in range(3):
        weights_ready(1, g)
        convert(1, g)
    z4_copy.wait()
    product([(tap_c, t, my_half) for t in range(9)], True)
    h_remote.wait_recv()
    for copy in out_copies[:2]:
        copy.wait()
    build_taps(fh.at[1], tap_a, items, pitch, boost, low.at[3])
    out_copies = out_copies[2:] + put_terms(tap_a, low.at[3], h0_out.at[other], 0)
    h_remote.wait_send()

    def outputs(start, count):
        for k in range(count):
            row = start + k
            z = acc[row] + bias5
            s = sigmoid(z)
            value = z * s
            for tile in range(tiles):
                fx[tile, row, pl.ds(HEAD, pitch)] = value[:, tile * LANES : (tile + 1) * LANES]
            a = base[0] + row * (per_pixel * SIDE % PRIME) % PRIME * 1.0
            a = jnp.where(a >= PRIME, a - PRIME, a)
            hashed = modulo(a * base[2] + base[1])
            cotangent = (hashed * (1.0 / 32760.0) - 1.0) * base[3]
            fh[0, row, pl.ds(HEAD, pitch)] = cotangent * (s * (1.0 + z * (1.0 - s)))

    product([(tap_a, t, theirs(half)) for t in range(9)], False)
    last = []
    for k, (begin, end) in enumerate(PARTS):
        pl.loop(begin, end)(lambda row: outputs(row, 1))
        rows = pl.ds(begin, end - begin)
        act = fx.at[pl.ds(0, tiles), rows, pl.ds(HEAD, pitch)]
        last.append(pltpu.make_async_copy(act, act_out.at[:, rows], o_sem.at[7 + 2 * k]))
        d5 = fh.at[0, rows, pl.ds(HEAD, pitch)]
        last.append(pltpu.make_async_copy(d5, d5_out.at[rows], o_sem.at[8 + 2 * k]))
        for copy in last[-2:]:
            copy.start()
    for copy in w_remote:
        copy.wait_send()
    rows_remote.wait()
    for copy in out_copies + last:
        copy.wait()


def forward(x, weights, biases, seeds, lengths, items, pitch):
    channels = x.shape[2]
    half = channels // 2
    tiles = half // LANES
    maps = (SIDE, pitch, half)
    tiled = jax.ShapeDtypeStruct((tiles, SIDE, pitch, LANES), F32)
    any_spec = pl.BlockSpec(memory_space=pl.ANY)
    smem = pl.BlockSpec(memory_space=pltpu.SMEM)
    taps = pltpu.VMEM((3, 2, SIDE + 2, pitch, half), BF16)
    staged = pltpu.VMEM((2, SIDE, HEAD + pitch + HEAD, half), F32)
    dma = pltpu.SemaphoreType.DMA
    terms = jax.ShapeDtypeStruct((2, 2) + maps, BF16)
    one = jax.ShapeDtypeStruct(maps, F32)
    return pl.pallas_call(
        functools.partial(forward_kernel, items, pitch),
        name="forward",
        out_shape=[tiled, one, one, terms, terms, jax.ShapeDtypeStruct((9, half, channels), F32)],
        in_specs=[smem, smem, any_spec, any_spec, any_spec],
        out_specs=[any_spec] * 6,
        scratch_shapes=[
            pltpu.VMEM(x.shape, F32),
            pltpu.VMEM((2 * tiles, SIDE, HEAD + pitch + HEAD, LANES), F32),
            staged, taps, taps, taps,
            pltpu.VMEM((4,) + maps, BF16),
            pltpu.VMEM((2, 9 * channels, half), F32),
            pltpu.VMEM((2, 9, channels, half), BF16),
            pltpu.VMEM(maps, F32),
            pltpu.VMEM((2, 1, channels), F32),
            pltpu.VMEM((5, pitch, half), F32),
            dma((2,)), dma((3,)), dma((3,)), dma((3,)), dma((2,)), dma((2,)), dma((3,)), dma((13,)),
        ],
        compiler_params=pltpu.CompilerParams(
            collective_id=0, has_side_effects=True, vmem_limit_bytes=62 * 2**20
        ),
    )(seeds, lengths, x, weights, biases)


LAG = 3
STEPS = 15
RING = 20


def exchange(n, own, r_first, r_line, r_last, fin, gx, wg, sems):
    sent, f_r, z_r, l_r, a_r, c_s, g_r, p_r = sems
    half = own.shape[1]
    part, chunk = half // 2, half // 8
    units = gx.shape[1] // half
    section, dp = lax.axis_index("section"), lax.axis_index("dp")
    x, y, z = lax.rem(dp, 2), lax.rem(lax.div(dp, 2), 2), lax.div(dp, 4)
    kind, slot = lax.rem(n, 2), lax.rem(n, RING)
    later = lax.div(n, units)
    layer, row0 = 1 - later, (n - later * units) * half
    keep = x + kind * (y - x)
    to_x, to_y = dp + 1 - 2 * x, dp + 2 - 4 * y
    first = {"dp": to_x + kind * (to_y - to_x)}
    last = {"dp": to_y + kind * (to_x - to_y)}
    up = {"dp": dp + 4 - 8 * lax.div(z, 3)}
    down = {"dp": dp - 4 + 8 * lax.div(3 - z, 3)}
    base = keep * part

    def rows(start, size):
        return pl.ds(pl.multiple_of(start, chunk), size)

    def remote(src, dst, recv, device):
        return pltpu.make_async_remote_copy(
            src, dst, sent.at[slot], recv, device_id=device, device_id_type=MESH
        )

    def first_copy():
        src = own.at[slot, rows((1 - keep) * part, part)]
        return remote(src, r_first.at[slot], f_r.at[slot], first)

    def line(way, lo, count):
        return remote(
            own.at[slot, rows(base + lo * chunk, count * chunk)],
            r_line.at[slot, way, pl.ds(lo * chunk, count * chunk)],
            z_r.at[slot, way], (up, down)[way],
        )

    def line_add(way, lo, count):
        line(way, lo, count).wait_recv()
        where = rows(base + lo * chunk, count * chunk)
        own[slot, where] += r_line[slot, way, pl.ds(lo * chunk, count * chunk)]

    def last_copy():
        src = own.at[slot, rows(base + z * chunk, chunk)]
        return remote(src, r_last.at[slot], l_r.at[slot], last)

    columns = pl.ds(pl.multiple_of(section * half, half), half)

    def home(body):
        @pl.when(layer == section)
        def _():
            body(lambda start, size: wg.at[rows(row0 + start, size), columns])

        @pl.when(layer != section)
        def _():
            body(lambda start, size: gx.at[layer, rows(row0 + start, size)])

    def spread(where, way, lo, count, src=None):
        dst = where(base + lo * chunk, count * chunk)
        return remote(dst if src is None else src, dst, a_r.at[slot, way], (up, down)[way])

    def keep_copy(where):
        return pltpu.make_async_copy(fin.at[slot], where(base + z * chunk, chunk), c_s.at[slot])

    def back_copy(where):
        kept = where(base, part)
        return remote(kept, kept, g_r.at[slot], first)

    def put_copy():
        unit, target = gx.at[layer, rows(row0, half)], wg.at[rows(row0, half), columns]
        return remote(unit, target, p_r.at[slot], {"section": 1 - section})

    def stage0():
        first_copy().start()

    def stage1():
        first_copy().wait_recv()
        own[slot, rows(base, part)] += r_first[slot]
        pl.when(z == 0)(lambda: line(0, 1, 3).start())
        pl.when(z == 3)(lambda: line(1, 0, 3).start())

    def stage2():
        @pl.when(z == 1)
        def _():
            line_add(0, 1, 3)
            line(0, 2, 2).start()

        @pl.when(z == 2)
        def _():
            line_add(1, 0, 3)
            line(1, 0, 2).start()

    def stage3():
        @pl.when(z == 1)
        def _():
            line_add(1, 0, 2)
            line(1, 0, 1).start()

        @pl.when(z == 2)
        def _():
            line_add(0, 2, 2)
            line(0, 3, 1).start()

    def stage4():
        pl.when(z == 0)(lambda: line_add(1, 0, 1))
        pl.when(z == 3)(lambda: line_add(0, 3, 1))
        last_copy().start()

    def stage5():
        last_copy().wait_recv()
        fin[slot] = own[slot, rows(base + z * chunk, chunk)] + r_last[slot]

        def body(where):
            keep_copy(where).start()
            pl.when(z == 0)(lambda: spread(where, 0, 0, 1, fin.at[slot]).start())
            pl.when(z == 3)(lambda: spread(where, 1, 3, 1, fin.at[slot]).start())

        home(body)

    def stage6():
        def body(where):
            @pl.when(z == 1)
            def _():
                keep_copy(where).wait()
                spread(where, 0, 0, 1).wait_recv()
                spread(where, 0, 0, 2).start()

            @pl.when(z == 2)
            def _():
                keep_copy(where).wait()
                spread(where, 1, 3, 1).wait_recv()
                spread(where, 1, 2, 2).start()

        home(body)

    def stage7():
        def body(where):
            @pl.when(z == 1)
            def _():
                spread(where, 1, 2, 2).wait_recv()
                spread(where, 1, 1, 3).start()

            @pl.when(z == 2)
            def _():
                spread(where, 0, 0, 2).wait_recv()
                spread(where, 0, 0, 3).start()

        home(body)

    def stage8():
        def body(where):
            @pl.when(z == 0)
            def _():
                keep_copy(where).wait()
                spread(where, 1, 1, 3).wait_recv()

            @pl.when(z == 3)
            def _():
                keep_copy(where).wait()
                spread(where, 0, 0, 3).wait_recv()

            back_copy(where).start()

        home(body)

    def stage9():
        home(lambda where: back_copy(where).wait_recv())
        pl.when(layer != section)(lambda: put_copy().start())

    def stage10():
        pl.when(layer == section)(lambda: put_copy().wait_recv())
        inner = (z == 1) | (z == 2)
        for middle, put, count in ((0, 0, 13), (0, 1, 21), (1, 0, 17), (1, 1, 25)):

            @pl.when((inner == (middle == 1)) & ((layer != section) == (put == 1)))
            def _(count=count):
                whole = gx.at[layer, pl.ds(0, count * chunk)]
                remote(whole, whole, p_r.at[slot], {"section": 1 - section}).wait_send()

    return [
        stage0, stage1, stage2, stage3, stage4, stage5, stage6, stage7, stage8, stage9, stage10,
    ]


OFFSETS = (0, 6, 10, 13, 16, 20, 23, 26, 29, 35, 37)


def backward_kernel(
    items, pitch, reduce,
    d5_hbm, z4_hbm, h0_hbm, x0_hbm, w_hbm, wr_hbm,
    gin_out, gx_out, wg_out, bg_out,
    fd, taps, feature, z4, acc, wstage, wbf, own, r_first, r_line, r_last, fin, b_send, b_recv, b_row,
    l_sem, dl_sem, w_sem, d_sem, bs_sem, br_sem, bo_sem, *sems,
):
    section, dp = lax.axis_index("section"), lax.axis_index("dp")
    other = 1 - section
    partner = {"section": other}
    half = acc.shape[2]
    units = 18
    x, y, z = dp % 2, dp // 2 % 2, dp // 4
    pairs = [{"dp": dp + 1 - 2 * x}, {"dp": dp + 2 - 4 * y}]
    pairs += [{"dp": dp + 4 - 8 * (z % 2)}, {"dp": dp + 8 - 16 * (z // 2)}]
    barrier = pltpu.get_barrier_semaphore()

    def greet(device):
        pl.semaphore_signal(barrier, inc=1, device_id=device, device_id_type=MESH)

    greet(partner)
    if reduce:
        for device in pairs:
            greet(device)
        pl.when(z == 1)(lambda: greet({"dp": dp + 4}))
        pl.when(z == 2)(lambda: greet({"dp": dp - 4}))

    def mine(width):
        return pl.ds(pl.multiple_of(section * width, width), width)

    d_local = []
    for k, (begin, end) in enumerate(PARTS):
        rows = pl.ds(begin, end - begin)
        dst = fd.at[0, rows, pl.ds(HEAD, pitch)]
        d_local.append(pltpu.make_async_copy(d5_hbm.at[rows], dst, dl_sem.at[k]))
    h_local = pltpu.make_async_copy(h0_hbm, feature.at[1], l_sem.at[1])
    z_local = pltpu.make_async_copy(z4_hbm, z4, l_sem.at[2])
    x_local = pltpu.make_async_copy(x0_hbm, feature.at[0], l_sem.at[3])
    for copy in d_local:
        copy.start()
    h_local.start()

    def w_copy(q, act):
        layer, slot = 1 - q // 3, q % 2
        three = pl.ds(q % 3 * 3, 3)
        whole = w_hbm.at[0].reshape(9, 2 * half, 2 * half)

        @pl.when(layer == section)
        def _():
            src = whole.at[three, mine(half)]
            act(pltpu.make_async_copy(src, wstage.at[slot], w_sem.at[slot]))

        @pl.when(layer != section)
        def _():
            act(pltpu.make_async_copy(wr_hbm.at[three], wstage.at[slot], w_sem.at[slot]))

    for k in range(3):
        clear_margins(fd.at[k], items, pitch)
    for k in range(3):
        clear_edges(taps.at[k])

    def d_remote(k):
        src = d5_hbm if k == 0 else fd.at[0, :, pl.ds(HEAD, pitch)]
        return pltpu.make_async_remote_copy(
            src, fd.at[1 + k, :, pl.ds(HEAD, pitch)],
            d_sem.at[k, 0], d_sem.at[k, 1], device_id=partner, device_id_type=MESH,
        )

    real = lax.broadcasted_iota(jnp.int32, (pitch, half), 0) < items * SIDE

    def column_sums():
        def add(row, total):
            v = fd[0, row, pl.ds(HEAD, pitch)]
            return total + jnp.sum(v.reshape(pitch // 8, 8, half), axis=0)

        return jnp.sum(lax.fori_loop(0, SIDE, add, jnp.zeros((8, half), F32)), axis=0, keepdims=True)

    for copy, span in zip(d_local, PARTS):
        copy.wait()
        build_taps(fd.at[0], taps.at[0], items, pitch, span=span)
    pl.semaphore_wait(barrier, 5 + (z + 1) // 2 % 2 if reduce else 1)
    d_remote(0).start()
    w_copy(0, lambda copy: copy.start())
    z_local.start()
    x_local.start()
    acc[...] = jnp.zeros_like(acc)
    h_local.wait()

    def first_sums():
        b_send[0, 0:8] = jnp.broadcast_to(column_sums(), (8, half))

    def enter(layer):
        z_local.wait()
        x_local.wait()

        @pl.loop(0, SIDE)
        def _(row):
            v = z4[row]
            s = sigmoid(v)
            d = acc[row] * (s * (1.0 + v * (1.0 - s)))
            fd[0, row, pl.ds(HEAD, pitch)] = jnp.where(real, d, 0.0)

        d_remote(1).start()
        build_taps(fd.at[0], taps.at[2], items, pitch)
        which = lax.broadcasted_iota(jnp.int32, (8, half), 0) == 0
        b_send[0] = jnp.where(which, jnp.broadcast_to(column_sums(), (8, half)), b_send[0])
        acc[...] = jnp.zeros_like(acc)

    def receive(k):
        d_remote(k).wait_recv()
        build_taps(fd.at[1 + k], taps.at[1], items, pitch)

    def kernel_unit(n):
        layer, step = 1 - n // units, n % units
        t, m = step // 2, step % 2
        row, col = 2 - t // 3, 2 - t % 3
        terms = ((0, 0), (1, 0), (0, 1))

        def contract(first, count):
            size = count * pitch
            v = [
                feature[layer, m, term, pl.ds(first, count)].reshape(size, half) for term in range(2)
            ]
            d = [
                taps[2 - 2 * layer, col, term, pl.ds(first + row, count)].reshape(size, half) for term in range(2)
            ]
            tail = size % 256
            cut = size - tail
            total = None
            for a, b in terms:
                part = dot_tn(v[a][:cut], d[b][:cut])
                total = part if total is None else total + part
            if tail:
                total += dot_tn(
                    jnp.concatenate([v[a][cut:] for a, b in terms], 0),
                    jnp.concatenate([d[b][cut:] for a, b in terms], 0),
                )
            own[n % RING] = total

        pl.when(row == 1)(lambda: contract(0, SIDE))
        pl.when(row != 1)(lambda: contract(jnp.where(row == 0, 1, 0), SIDE - 1))

    def input_piece(layer, p):
        g, j = p // 6, p % 6
        q = 3 * (1 - layer) + g

        @pl.when(j == 0)
        def _():
            w_copy(q, lambda copy: copy.wait())
            pl.when(q + 1 < 6)(lambda: w_copy(q + 1, lambda copy: copy.start()))
            for k in range(3):
                wbf[0, k], wbf[1, k] = split(wstage[q % 2, k])

        def tile(start, count):
            total = None
            for h in range(2):
                for k in range(3):
                    for a, b in ((0, 0), (1, 0), (0, 1)):
                        v = taps[1 if h else 2 - 2 * layer, 2 - k, a, pl.ds(start + 2 - g, count)]
                        w = wbf[b, k, :, pl.ds(pl.multiple_of((section + h) % 2 * half, half), half)]
                        part = dot_nt(v.reshape(count * pitch, half), w)
                        total = part if total is None else total + part
            acc[pl.ds(start, count)] += total.reshape(count, pitch, half)

        top, bottom = (j == 0) & (g == 2), (j == 5) & (g == 0)
        pl.when((j < 5) & jnp.logical_not(top))(lambda: tile(2 * j, 2))
        pl.when(top)(lambda: tile(1, 1))
        pl.when((j == 5) & (g != 0))(lambda: tile(10, SIDE - 10))
        pl.when(bottom)(lambda: tile(10, SIDE - 11))

    def bias_copy(k, device):
        return pltpu.make_async_remote_copy(
            b_send.at[k], b_recv.at[k], bs_sem.at[k], br_sem.at[k], device_id=device, device_id_type=MESH
        )

    put_row = pltpu.make_async_copy(b_row, bg_out, bo_sem.at[0])

    def bias_step(k):
        if k > 0 and k < 5:
            bias_copy(k - 1, pairs[k - 1]).wait_recv()
            b_send[k] = b_send[k - 1] + b_recv[k - 1]
        if k < 4:
            bias_copy(k, pairs[k]).start()
        if k == 4:
            bias_copy(4, partner).start()
        if k == 5:
            bias_copy(4, partner).wait_recv()
            for s in range(2):

                @pl.when(section == s)
                def _(s=s):
                    b_row[:, s * half : (s + 1) * half] = b_send[4, s : s + 1]
                    b_row[:, (1 - s) * half : (2 - s) * half] = b_recv[4, s : s + 1]

            put_row.start()

    tiles = half // LANES
    put_acc = [
        pltpu.make_async_copy(
            acc.at[:, :, pl.ds(tile * LANES, LANES)], gin_out.at[tile], l_sem.at[4 + tile]
        )
        for tile in range(tiles)
    ]

    def local_part(n):
        layer, row0 = 1 - n // units, n % units * half
        dst = gx_out.at[layer, pl.ds(pl.multiple_of(row0, half), half)]
        return pltpu.make_async_copy(own.at[n % RING], dst, sems[0].at[n % RING])

    def service(u, odd):
        for k, offset in enumerate(OFFSETS):
            if k == 0 or offset % 2 != odd:
                continue
            valid, n = unit_of(u - offset // 2)

            @pl.when(valid)
            def _():
                stages = exchange(n, own, r_first, r_line, r_last, fin, gx_out, wg_out, sems)
                stages[k]()

    lag = LAG
    turn = lag + STEPS
    late0 = turn + lag
    last = 2 * units + (OFFSETS[-1] + 1) // 2

    def unit_of(u):
        return (u >= 0) & (u < 2 * units), u

    @pl.loop(0, last)
    def _(u):
        valid, n = unit_of(u)
        pl.when(u == lag)(lambda: receive(0))
        pl.when(u == 2)(lambda: first_sums())
        pl.when(u == turn)(lambda: enter(0))
        pl.when(u == late0)(lambda: receive(1))

        @pl.when(valid)
        def _():
            if not reduce:
                pl.when(n >= RING)(lambda: local_part(n - RING).wait())
            kernel_unit(n)
            if reduce:
                exchange(n, own, r_first, r_line, r_last, fin, gx_out, wg_out, sems)[0]()
            else:
                local_part(n).start()

        if reduce:
            service(u, 0)
        early = (u >= lag) & (u < turn)
        late = (u >= late0) & (u < late0 + units)

        done = jnp.where(early, lax.div((u - lag) * units, STEPS), u - late0)
        upto = jnp.where(early, lax.div((u - lag + 1) * units, STEPS), done + 1)

        @pl.loop(0, jnp.where(early | late, upto - done, 0))
        def _(i):
            input_piece(jnp.where(early, 1, 0), done + i)

        @pl.when(u == late0 + units - 1)
        def _():
            for copy in put_acc:
                copy.start()

        if reduce:
            service(u, 1)
        for k in range(6 if reduce else 0):
            pl.when(u == turn + 2 + 2 * k)(lambda k=k: bias_step(k))

    if not reduce:

        @pl.loop(2 * units - RING, 2 * units)
        def _(n):
            local_part(n).wait()

    if reduce:
        for k in range(5):
            bias_copy(k, (pairs + [partner])[k]).wait_send()
        put_row.wait()
    else:
        put_sums = pltpu.make_async_copy(b_send.at[0], bg_out, bo_sem.at[0])
        put_sums.start()
        put_sums.wait()
    for k in range(2):
        d_remote(k).wait_send()
    for copy in put_acc:
        copy.wait()


def backward(d5, z4, h0, x0, weights, rows_other, items, reduce):
    maps = d5.shape
    _, pitch, half = maps
    channels = 2 * half
    any_spec = pl.BlockSpec(memory_space=pl.ANY)
    dma = pltpu.SemaphoreType.DMA
    shape = jax.ShapeDtypeStruct
    ring = RING
    part, chunk = half // 2, half // 8
    return pl.pallas_call(
        functools.partial(backward_kernel, items, pitch, reduce),
        name="backward",
        out_shape=[
            shape((half // LANES, SIDE, pitch, LANES), F32),
            shape((2, 9 * channels, half), F32),
            shape((9 * channels, channels), F32),
            shape((1, channels) if reduce else (8, half), F32),
        ],
        in_specs=[any_spec] * 6,
        out_specs=[any_spec] * 4,
        scratch_shapes=[
            pltpu.VMEM((3, SIDE, HEAD + pitch + HEAD, half), F32),
            pltpu.VMEM((3, 3, 2, SIDE + 2, pitch, half), BF16),
            pltpu.VMEM((2, 2, 2) + maps, BF16),
            pltpu.VMEM(maps, F32),
            pltpu.VMEM(maps, F32),
            pltpu.VMEM((2, 3, half, channels), F32),
            pltpu.VMEM((2, 3, half, channels), BF16),
            pltpu.VMEM((ring, half, half), F32),
            pltpu.VMEM((ring, part, half), F32),
            pltpu.VMEM((ring, 2, part, half), F32),
            pltpu.VMEM((ring, chunk, half), F32),
            pltpu.VMEM((ring, chunk, half), F32),
            pltpu.VMEM((5, 8, half), F32),
            pltpu.VMEM((5, 8, half), F32),
            pltpu.VMEM((1, channels), F32),
            dma((4 + half // LANES,)), dma((len(PARTS),)), dma((2,)), dma((2, 2)), dma((5,)), dma((5,)), dma((1,)),
            dma((ring,)), dma((ring,)), dma((ring, 2)), dma((ring,)), dma((ring, 2)), dma((ring,)),
            dma((ring,)), dma((ring,)),
        ],
        compiler_params=pltpu.CompilerParams(
            collective_id=1, has_side_effects=True, vmem_limit_bytes=62 * 2**20
        ),
    )(d5, z4, h0, x0, weights, rows_other)


def finish_kernel(
    items, rows_in, act_hbm, gin_hbm, wg_hbm, bias_hbm, act_out, gin_out, wg_out, bias_out,
    act_rows, gin_rows, act, gin, wg, bias, i_sem, o_sem,
):
    pieces = wg.shape[0] // rows_in
    count = pieces + 3

    def incoming(k):
        if k < 2:
            src, dst = ((act_hbm, act_rows), (gin_hbm, gin_rows))[k]
        elif k == count - 1:
            src, dst = bias_hbm, bias
        else:
            rows = pl.ds((k - 2) * rows_in, rows_in)
            src, dst = wg_hbm.at[rows], wg.at[rows]
        return pltpu.make_async_copy(src, dst, i_sem.at[k])

    def outgoing(k):
        if k < 2:
            src, dst = ((act, act_out), (gin, gin_out))[k]
        elif k == count - 1:
            src, dst = bias, bias_out
        else:
            rows = pl.ds((k - 2) * rows_in, rows_in)
            src, dst = wg.at[rows], wg_out.at[0, rows]
        return pltpu.make_async_copy(src, dst, o_sem.at[k])

    for k in range(count):
        incoming(k).start()
    for k, (rows, maps) in enumerate(((act_rows, act), (gin_rows, gin))):
        incoming(k).wait()
        for row in range(SIDE):
            for n in range(items):
                for tile in range(rows.shape[0]):
                    maps[
                        n, row * SIDE : (row + 1) * SIDE, tile * LANES : (tile + 1) * LANES
                    ] = rows[tile, row, pl.ds(n, SIDE, stride=items), :]
        outgoing(k).start()
        for j in range(pieces):
            if j % 2 == k:
                incoming(2 + j).wait()
                outgoing(2 + j).start()
    incoming(count - 1).wait()
    outgoing(count - 1).start()
    for k in range(count):
        outgoing(k).wait()


def finish(act, gin, wg, bias, items):
    half = act.shape[0] * LANES
    any_spec = pl.BlockSpec(memory_space=pl.ANY)
    maps = (items, SIDE * SIDE, half)
    pieces = 6
    dma = pltpu.SemaphoreType.DMA
    return pl.pallas_call(
        functools.partial(finish_kernel, items, wg.shape[0] // pieces),
        name="finish",
        out_shape=[
            jax.ShapeDtypeStruct(maps, F32),
            jax.ShapeDtypeStruct(maps, F32),
            jax.ShapeDtypeStruct((1,) + wg.shape, F32),
            jax.ShapeDtypeStruct(bias.shape, F32),
        ],
        in_specs=[any_spec] * 4,
        out_specs=[any_spec] * 4,
        scratch_shapes=[
            pltpu.VMEM(act.shape, F32),
            pltpu.VMEM(act.shape, F32),
            pltpu.VMEM(maps, F32),
            pltpu.VMEM(maps, F32),
            pltpu.VMEM(wg.shape, F32),
            pltpu.VMEM(bias.shape, F32),
            dma((pieces + 3,)),
            dma((pieces + 3,)),
        ],
        compiler_params=pltpu.CompilerParams(vmem_limit_bytes=62 * 2**20),
    )(act, gin, wg, bias)


def per_device(flow_maps, weights, biases, stack_lengths, grad_seeds):
    items = flow_maps.shape[0]
    channels = flow_maps.shape[2]
    half = channels // 2
    pitch = ceil_to(items * SIDE, 16)
    section = lax.axis_index("section")
    act, z4, d5, h0, x0, rows_other = forward(
        flow_maps, weights, biases, grad_seeds, stack_lengths, items, pitch
    )
    fused = lax.axis_size("dp") == 16
    gin, parts, grad, bias = backward(d5, z4, h0, x0, weights, rows_other, items, fused)
    if not fused:
        parts, bias = lax.psum((parts, bias[:2]), "dp")
        given = lax.dynamic_index_in_dim(parts, 1 - section, 0, keepdims=False)
        kept = lax.dynamic_index_in_dim(parts, section, 0, keepdims=False)
        got = lax.ppermute(given, "section", [(0, 1), (1, 0)])
        first, second = jnp.where(section == 0, kept, got), jnp.where(section == 0, got, kept)
        grad = jnp.concatenate([first, second], axis=1)
        both = lax.all_gather(bias, "section", axis=1, tiled=True)
        bias = lax.dynamic_index_in_dim(both, section, 0)
    act, gin, grad, bias = finish(act, gin, grad, bias, items)
    return (act, gin, grad, bias)


def solution(mesh):
    in_specs = (P("dp", None, None), P("section", None, None), P("section", None), P("dp"), P("dp"))
    out_specs = (
        P("dp", None, "section"),
        P("dp", None, "section"),
        P("section", None, None),
        P("section", None),
    )
    return jax.shard_map(
        per_device, mesh=mesh, in_specs=in_specs, out_specs=out_specs, check_vma=False
    )
```

```python
import functools

import jax
import jax.numpy as jnp
from jax import lax
from jax.experimental import pallas as pl
from jax.experimental.pallas import tpu as pltpu
from jax.sharding import PartitionSpec as P

SIDE = 13
PRIME = 65521
F32, BF16 = jnp.float32, jnp.bfloat16
MESH = pl.DeviceIdType.MESH
LANES = 128
PARTS = ((0, 5), (5, 9), (9, SIDE))
HEAD = 16


def ceil_to(value, unit):
    return -(-value // unit) * unit


def split(v):
    hi = v.astype(BF16)
    return hi, (v - hi.astype(F32)).astype(BF16)


BOOST = 32.0


def boost(v):
    hi = v.astype(BF16)
    wide = hi.astype(F32)
    return hi, (wide + (v - wide) * BOOST).astype(BF16)


def dot(a, b):
    return jnp.dot(a, b, preferred_element_type=F32)


def dot_nt(a, b):
    return lax.dot_general(a, b, (((1,), (1,)), ((), ())), preferred_element_type=F32)


def dot_tn(a, b):
    return lax.dot_general(a, b, (((0,), (0,)), ((), ())), preferred_element_type=F32)


def modulo(v):
    quotient = jnp.floor(v * (1.0 / PRIME) - 1e-4)
    rest = v - quotient * PRIME
    return jnp.where(rest >= PRIME, rest - PRIME, rest)


def clear_margins(staged, items, pitch):
    zeros = jnp.zeros((SIDE, HEAD, staged.shape[2]), F32)
    staged[:, 0:HEAD, :] = zeros
    staged[:, HEAD + pitch : HEAD + pitch + HEAD, :] = zeros


def clear_edges(taps):
    zeros = jnp.zeros(taps.shape[:2] + taps.shape[3:], BF16)
    taps[:, :, 0] = zeros
    taps[:, :, SIDE + 1] = zeros


def build_taps(staged, taps, items, pitch, terms=split, low=None, span=(0, SIDE)):
    @pl.loop(*span)
    def _(row):
        build_row(staged, taps, row, items, pitch, terms, low)


def build_row(staged, taps, row, items, pitch, terms=split, low=None):
    for col in range(3):
        start = HEAD + (col - 1) * items
        v = staged[row, start : start + pitch, :]
        taps[col, 0, row + 1], taps[col, 1, row + 1] = terms(v)
        if low is not None and col == 1:
            low[row] = split(v)[1]


def gather_rows(maps, staged, items):
    for row in range(SIDE):
        for n in range(items):
            for tile in range(staged.shape[0]):
                staged[tile, row, pl.ds(HEAD + n, SIDE, stride=items), :] = maps[
                    n, row * SIDE : (row + 1) * SIDE, tile * LANES : (tile + 1) * LANES
                ]


def build_tiled(staged, taps, items, pitch, low):
    @pl.loop(0, SIDE)
    def _(row):
        for col in range(3):
            start = HEAD + (col - 1) * items
            for tile in range(staged.shape[0]):
                v = staged[tile, row, start : start + pitch, :]
                lanes = slice(tile * LANES, (tile + 1) * LANES)
                taps[col, 0, row + 1, :, lanes], taps[col, 1, row + 1, :, lanes] = boost(v)
                if col == 1:
                    low[row, :, lanes] = split(v)[1]


def window(taps, col, term, row):
    piece = taps[col, term, pl.ds(row, SIDE)]
    return piece.reshape(piece.shape[0] * piece.shape[1], piece.shape[2])


def each_tile(body, count=4):
    whole = SIDE // count

    @pl.loop(0, whole)
    def _(k):
        body(k * count, count)

    if SIDE % count:
        body(whole * count, SIDE % count)


def sigmoid(z):
    below = 1.0 + jnp.exp(-jnp.maximum(z, -80.0))
    guess = pl.reciprocal(below, approx=True)
    return guess * (2.0 - below * guess)


def forward_kernel(
    items, pitch,
    seeds, lengths, x_hbm, w_hbm, b_hbm,
    act_out, z4_out, d5_out, h0_out, x0_out, wr_out,
    maps, fx, fh, tap_a, tap_b, tap_c, low, wstage, wbf, acc, bias, base,
    x_sem, wl_sem, ws_sem, wr_sem, row_sem, h_sem, b_sem, o_sem,
):
    section = lax.axis_index("section")
    other = 1 - section
    partner = {"section": other}
    half = acc.shape[2]
    taps3 = 3 * 2 * half
    barrier = pltpu.get_barrier_semaphore()
    pl.semaphore_signal(barrier, inc=1, device_id=partner, device_id_type=MESH)

    def mine(width):
        return pl.ds(pl.multiple_of(section * width, width), width)

    def theirs(width):
        return pl.ds(pl.multiple_of(other * width, width), width)

    x_copies = [
        pltpu.make_async_copy(
            x_hbm.at[:, :, pl.ds(h * half, half)], maps.at[:, :, pl.ds(h * half, half)], x_sem.at[h]
        )
        for h in range(2)
    ]
    for copy in x_copies:
        copy.start()
    w_local, w_remote = [], []
    for g in range(3):
        rows = pl.ds(g * taps3, taps3)
        w_local.append(
            pltpu.make_async_copy(
                w_hbm.at[0, rows, mine(half)], wstage.at[section, rows], wl_sem.at[g]
            )
        )
        w_remote.append(
            pltpu.make_async_remote_copy(
                w_hbm.at[0, rows, theirs(half)], wstage.at[section, rows],
                ws_sem.at[g], wr_sem.at[g], device_id=partner, device_id_type=MESH,
            )
        )
    for copy in w_local:
        copy.start()
    b_local = pltpu.make_async_copy(b_hbm, bias.at[section], b_sem.at[0])
    b_local.start()
    pl.semaphore_wait(barrier, 1)
    b_remote = pltpu.make_async_remote_copy(
        b_hbm, bias.at[section], b_sem.at[1], b_sem.at[2], device_id=partner, device_id_type=MESH
    )
    b_remote.start()
    for copy in w_remote:
        copy.start()
    rows_remote = pltpu.make_async_remote_copy(
        w_hbm.at[0].reshape(9, 2 * half, 2 * half).at[:, theirs(half)], wr_out,
        row_sem.at[0], row_sem.at[1], device_id=partner, device_id_type=MESH,
    )
    rows_remote.start()

    for taps in (tap_a, tap_b, tap_c):
        clear_edges(taps)
    tiles = half // LANES
    for tile in range(2 * tiles):
        fx[tile] = jnp.zeros(fx.shape[1:], F32)
    for h in range(2):
        clear_margins(fh.at[h], items, pitch)

    item_of = lax.broadcasted_iota(jnp.int32, (pitch, half), 0)
    column = jnp.floor((item_of.astype(F32) + 0.5) * (1.0 / items))
    item_row = item_of.astype(F32) - column * items
    seed_rows = jnp.zeros((pitch, half), F32)
    factor_rows = jnp.zeros((pitch, half), F32)
    scale_rows = jnp.zeros((pitch, half), F32)
    for n in range(items):
        hit = item_row == float(n)
        seed = seeds[n]
        seed_rows = jnp.where(hit, seed.astype(F32), seed_rows)
        factor_rows = jnp.where(hit, (seed % 251 + 2).astype(F32), factor_rows)
        scale_rows = jnp.where(hit, lengths[n].astype(F32) * 0.1, scale_rows)
    channel = lax.broadcasted_iota(jnp.int32, (pitch, half), 1) + section * half
    per_pixel = 7919 * 2 * half % PRIME
    base[0] = modulo(column * per_pixel + channel.astype(F32) * 7919.0)
    base[1] = seed_rows
    base[2] = factor_rows
    real = base.at[4]
    real[...] = jnp.where(item_of < items * SIDE, 1.0, 0.0)
    base[3] = scale_rows * real[...]

    out_copies = []

    def put_terms(taps, rest, out, k):
        copies = [
            pltpu.make_async_copy(taps.at[1, 0, pl.ds(1, SIDE)], out.at[0], o_sem.at[2 * k]),
            pltpu.make_async_copy(rest, out.at[1], o_sem.at[2 * k + 1]),
        ]
        for copy in copies:
            copy.start()
        return copies

    for h, taps in ((0, tap_a), (1, tap_b)):
        x_copies[h].wait()
        staged = fx.at[pl.ds(h * tiles, tiles)]
        gather_rows(maps.at[:, :, pl.ds(h * half, half)], staged, items)
        build_tiled(staged, taps, items, pitch, low.at[h])
        out_copies += put_terms(taps, low.at[h], x0_out.at[h], h)
    b_local.wait()
    b_remote.wait()

    def weights_ready(layer, g):
        @pl.when(section == layer)
        def _():
            w_local[g].wait()

        @pl.when(section != layer)
        def _():
            w_remote[g].wait_recv()

    def convert(layer, g):
        for k in range(3):
            t = g * 3 + k
            rows = pl.ds(t * 2 * half, 2 * half)
            if not isinstance(t, int):
                rows = pl.ds(pl.multiple_of(t * 2 * half, 2 * half), 2 * half)
            wbf[0, t], wbf[1, t] = boost(wstage[layer, rows, :])

    def product(parts, first):
        def tile(start, count):
            totals = [None, None]
            for taps, t, rows in parts:
                row, col = t // 3, t % 3
                if row == 2 and isinstance(start, int) and start == SIDE - 1:
                    continue
                for a in range(2):
                    v = taps[col, a, pl.ds(start + row, count)].reshape(count * pitch, half)
                    term = dot(v, wbf[a, t, rows, :])
                    totals[a] = term if totals[a] is None else totals[a] + term
            if totals[0] is None:
                return
            total = totals[0] + (totals[1] - totals[0]) * (1.0 / BOOST)
            total = total.reshape(count, pitch, half)
            where = pl.ds(start, count)
            acc[where] = total if first else acc[where] + total

        each_tile(tile)

    my_half = mine(half)
    bias4, bias5 = bias[0, :, my_half], bias[1, :, my_half]

    def hidden(start, count):
        for k in range(count):
            row = start + k
            z = acc[row] + bias4
            acc[row] = z
            fh[0, row, pl.ds(HEAD, pitch)] = z * sigmoid(z) * real[...]
            build_row(fh.at[0], tap_c, row, items, pitch, boost, low.at[2])

    for g in range(3):
        weights_ready(0, g)
        convert(0, g)
        product(
            [
                (taps, g * 3 + k, slice(h * half, (h + 1) * half))
                for h, taps in ((0, tap_a), (1, tap_b))
                for k in range(3)
            ],
            g == 0,
        )

    h_remote = pltpu.make_async_remote_copy(
        fh.at[0, :, pl.ds(HEAD, pitch)], fh.at[1, :, pl.ds(HEAD, pitch)],
        h_sem.at[0], h_sem.at[1], device_id=partner, device_id_type=MESH,
    )
    pl.loop(0, SIDE)(lambda row: hidden(row, 1))
    h_remote.start()
    z4_copy = pltpu.make_async_copy(acc, z4_out, o_sem.at[6])
    z4_copy.start()
    out_copies += put_terms(tap_c, low.at[2], h0_out.at[section], 2)
    for g in range(3):
        weights_ready(1, g)
        convert(1, g)
    z4_copy.wait()
    product([(tap_c, t, my_half) for t in range(9)], True)
    h_remote.wait_recv()
    for copy in out_copies[:2]:
        copy.wait()
    build_taps(fh.at[1], tap_a, items, pitch, boost, low.at[3])
    out_copies = out_copies[2:] + put_terms(tap_a, low.at[3], h0_out.at[other], 0)
    h_remote.wait_send()

    def outputs(start, count):
        for k in range(count):
            row = start + k
            z = acc[row] + bias5
            s = sigmoid(z)
            value = z * s
            for tile in range(tiles):
                fx[tile, row, pl.ds(HEAD, pitch)] = value[:, tile * LANES : (tile + 1) * LANES]
            a = base[0] + row * (per_pixel * SIDE % PRIME) % PRIME * 1.0
            a = jnp.where(a >= PRIME, a - PRIME, a)
            hashed = modulo(a * base[2] + base[1])
            cotangent = (hashed * (1.0 / 32760.0) - 1.0) * base[3]
            fh[0, row, pl.ds(HEAD, pitch)] = cotangent * (s * (1.0 + z * (1.0 - s)))

    product([(tap_a, t, theirs(half)) for t in range(9)], False)
    last = []
    for k, (begin, end) in enumerate(PARTS):
        pl.loop(begin, end)(lambda row: outputs(row, 1))
        rows = pl.ds(begin, end - begin)
        act = fx.at[pl.ds(0, tiles), rows, pl.ds(HEAD, pitch)]
        last.append(pltpu.make_async_copy(act, act_out.at[:, rows], o_sem.at[7 + 2 * k]))
        d5 = fh.at[0, rows, pl.ds(HEAD, pitch)]
        last.append(pltpu.make_async_copy(d5, d5_out.at[rows], o_sem.at[8 + 2 * k]))
        for copy in last[-2:]:
            copy.start()
    for copy in w_remote:
        copy.wait_send()
    rows_remote.wait()
    for copy in out_copies + last:
        copy.wait()


def forward(x, weights, biases, seeds, lengths, items, pitch):
    channels = x.shape[2]
    half = channels // 2
    tiles = half // LANES
    maps = (SIDE, pitch, half)
    tiled = jax.ShapeDtypeStruct((tiles, SIDE, pitch, LANES), F32)
    any_spec = pl.BlockSpec(memory_space=pl.ANY)
    smem = pl.BlockSpec(memory_space=pltpu.SMEM)
    taps = pltpu.VMEM((3, 2, SIDE + 2, pitch, half), BF16)
    staged = pltpu.VMEM((2, SIDE, HEAD + pitch + HEAD, half), F32)
    dma = pltpu.SemaphoreType.DMA
    terms = jax.ShapeDtypeStruct((2, 2) + maps, BF16)
    one = jax.ShapeDtypeStruct(maps, F32)
    return pl.pallas_call(
        functools.partial(forward_kernel, items, pitch),
        name="forward",
        out_shape=[tiled, one, one, terms, terms, jax.ShapeDtypeStruct((9, half, channels), F32)],
        in_specs=[smem, smem, any_spec, any_spec, any_spec],
        out_specs=[any_spec] * 6,
        scratch_shapes=[
            pltpu.VMEM(x.shape, F32),
            pltpu.VMEM((2 * tiles, SIDE, HEAD + pitch + HEAD, LANES), F32),
            staged, taps, taps, taps,
            pltpu.VMEM((4,) + maps, BF16),
            pltpu.VMEM((2, 9 * channels, half), F32),
            pltpu.VMEM((2, 9, channels, half), BF16),
            pltpu.VMEM(maps, F32),
            pltpu.VMEM((2, 1, channels), F32),
            pltpu.VMEM((5, pitch, half), F32),
            dma((2,)), dma((3,)), dma((3,)), dma((3,)), dma((2,)), dma((2,)), dma((3,)), dma((13,)),
        ],
        compiler_params=pltpu.CompilerParams(
            collective_id=0, has_side_effects=True, vmem_limit_bytes=62 * 2**20
        ),
    )(seeds, lengths, x, weights, biases)


LAG = 3
STEPS = 15
RING = 20


def exchange(n, own, r_first, r_line, r_last, fin, gx, wg, sems):
    sent, f_r, z_r, l_r, a_r, c_s, g_r, p_r = sems
    half = own.shape[1]
    part, chunk = half // 2, half // 8
    units = gx.shape[1] // half
    section, dp = lax.axis_index("section"), lax.axis_index("dp")
    x, y, z = lax.rem(dp, 2), lax.rem(lax.div(dp, 2), 2), lax.div(dp, 4)
    kind, slot = lax.rem(n, 2), lax.rem(n, RING)
    later = lax.div(n, units)
    layer, row0 = 1 - later, (n - later * units) * half
    keep = x + kind * (y - x)
    to_x, to_y = dp + 1 - 2 * x, dp + 2 - 4 * y
    first = {"dp": to_x + kind * (to_y - to_x)}
    last = {"dp": to_y + kind * (to_x - to_y)}
    up = {"dp": dp + 4 - 8 * lax.div(z, 3)}
    down = {"dp": dp - 4 + 8 * lax.div(3 - z, 3)}
    base = keep * part

    def rows(start, size):
        return pl.ds(pl.multiple_of(start, chunk), size)

    def remote(src, dst, recv, device):
        return pltpu.make_async_remote_copy(
            src, dst, sent.at[slot], recv, device_id=device, device_id_type=MESH
        )

    def first_copy():
        src = own.at[slot, rows((1 - keep) * part, part)]
        return remote(src, r_first.at[slot], f_r.at[slot], first)

    def line(way, lo, count):
        return remote(
            own.at[slot, rows(base + lo * chunk, count * chunk)],
            r_line.at[slot, way, pl.ds(lo * chunk, count * chunk)],
            z_r.at[slot, way], (up, down)[way],
        )

    def line_add(way, lo, count):
        line(way, lo, count).wait_recv()
        where = rows(base + lo * chunk, count * chunk)
        own[slot, where] += r_line[slot, way, pl.ds(lo * chunk, count * chunk)]

    def last_copy():
        src = own.at[slot, rows(base + z * chunk, chunk)]
        return remote(src, r_last.at[slot], l_r.at[slot], last)

    columns = pl.ds(pl.multiple_of(section * half, half), half)

    def home(body):
        @pl.when(layer == section)
        def _():
            body(lambda start, size: wg.at[rows(row0 + start, size), columns])

        @pl.when(layer != section)
        def _():
            body(lambda start, size: gx.at[layer, rows(row0 + start, size)])

    def spread(where, way, lo, count, src=None):
        dst = where(base + lo * chunk, count * chunk)
        return remote(dst if src is None else src, dst, a_r.at[slot, way], (up, down)[way])

    def keep_copy(where):
        return pltpu.make_async_copy(fin.at[slot], where(base + z * chunk, chunk), c_s.at[slot])

    def back_copy(where):
        kept = where(base, part)
        return remote(kept, kept, g_r.at[slot], first)

    def put_copy():
        unit, target = gx.at[layer, rows(row0, half)], wg.at[rows(row0, half), columns]
        return remote(unit, target, p_r.at[slot], {"section": 1 - section})

    def stage0():
        first_copy().start()

    def stage1():
        first_copy().wait_recv()
        own[slot, rows(base, part)] += r_first[slot]
        pl.when(z == 0)(lambda: line(0, 1, 3).start())
        pl.when(z == 3)(lambda: line(1, 0, 3).start())

    def stage2():
        @pl.when(z == 1)
        def _():
            line_add(0, 1, 3)
            line(0, 2, 2).start()

        @pl.when(z == 2)
        def _():
            line_add(1, 0, 3)
            line(1, 0, 2).start()

    def stage3():
        @pl.when(z == 1)
        def _():
            line_add(1, 0, 2)
            line(1, 0, 1).start()
            last_copy().start()

        @pl.when(z == 2)
        def _():
            line_add(0, 2, 2)
            line(0, 3, 1).start()
            last_copy().start()

    def stage4():
        @pl.when(z == 0)
        def _():
            line_add(1, 0, 1)
            last_copy().start()

        @pl.when(z == 3)
        def _():
            line_add(0, 3, 1)
            last_copy().start()

    def stage5():
        last_copy().wait_recv()
        fin[slot] = own[slot, rows(base + z * chunk, chunk)] + r_last[slot]

        def body(where):
            keep_copy(where).start()
            pl.when(z == 0)(lambda: spread(where, 0, 0, 1, fin.at[slot]).start())
            pl.when(z == 3)(lambda: spread(where, 1, 3, 1, fin.at[slot]).start())

        home(body)

    def stage6():
        def body(where):
            @pl.when(z == 1)
            def _():
                keep_copy(where).wait()
                spread(where, 0, 0, 1).wait_recv()
                spread(where, 0, 0, 2).start()

            @pl.when(z == 2)
            def _():
                keep_copy(where).wait()
                spread(where, 1, 3, 1).wait_recv()
                spread(where, 1, 2, 2).start()

        home(body)

    def stage7():
        def body(where):
            @pl.when(z == 1)
            def _():
                spread(where, 1, 2, 2).wait_recv()
                spread(where, 1, 1, 3).start()
                back_copy(where).start()

            @pl.when(z == 2)
            def _():
                spread(where, 0, 0, 2).wait_recv()
                spread(where, 0, 0, 3).start()
                back_copy(where).start()

        home(body)

    def stage8():
        def body(where):
            @pl.when(z == 0)
            def _():
                keep_copy(where).wait()
                spread(where, 1, 1, 3).wait_recv()
                back_copy(where).start()

            @pl.when(z == 3)
            def _():
                keep_copy(where).wait()
                spread(where, 0, 0, 3).wait_recv()
                back_copy(where).start()

        home(body)

    def stage9():
        home(lambda where: back_copy(where).wait_recv())
        pl.when(layer != section)(lambda: put_copy().start())

    def stage10():
        pl.when(layer == section)(lambda: put_copy().wait_recv())
        inner = (z == 1) | (z == 2)
        for middle, put, count in ((0, 0, 13), (0, 1, 21), (1, 0, 17), (1, 1, 25)):

            @pl.when((inner == (middle == 1)) & ((layer != section) == (put == 1)))
            def _(count=count):
                whole = gx.at[layer, pl.ds(0, count * chunk)]
                remote(whole, whole, p_r.at[slot], {"section": 1 - section}).wait_send()

    return [
        stage0, stage1, stage2, stage3, stage4, stage5, stage6, stage7, stage8, stage9, stage10,
    ]


OFFSETS = (0, 6, 10, 13, 16, 20, 23, 26, 29, 35, 37)


def backward_kernel(
    items, pitch, reduce,
    d5_hbm, z4_hbm, h0_hbm, x0_hbm, w_hbm, wr_hbm,
    gin_out, gx_out, wg_out, bg_out,
    fd, taps, feature, z4, acc, wstage, wbf, own, r_first, r_line, r_last, fin, b_send, b_recv, b_row,
    l_sem, dl_sem, w_sem, d_sem, bs_sem, br_sem, bo_sem, *sems,
):
    section, dp = lax.axis_index("section"), lax.axis_index("dp")
    other = 1 - section
    partner = {"section": other}
    half = acc.shape[2]
    units = 18
    x, y, z = dp % 2, dp // 2 % 2, dp // 4
    pairs = [{"dp": dp + 1 - 2 * x}, {"dp": dp + 2 - 4 * y}]
    pairs += [{"dp": dp + 4 - 8 * (z % 2)}, {"dp": dp + 8 - 16 * (z // 2)}]
    barrier = pltpu.get_barrier_semaphore()

    def greet(device):
        pl.semaphore_signal(barrier, inc=1, device_id=device, device_id_type=MESH)

    greet(partner)
    if reduce:
        for device in pairs:
            greet(device)
        pl.when(z == 1)(lambda: greet({"dp": dp + 4}))
        pl.when(z == 2)(lambda: greet({"dp": dp - 4}))

    def mine(width):
        return pl.ds(pl.multiple_of(section * width, width), width)

    d_local = []
    for k, (begin, end) in enumerate(PARTS):
        rows = pl.ds(begin, end - begin)
        dst = fd.at[0, rows, pl.ds(HEAD, pitch)]
        d_local.append(pltpu.make_async_copy(d5_hbm.at[rows], dst, dl_sem.at[k]))
    h_local = pltpu.make_async_copy(h0_hbm, feature.at[1], l_sem.at[1])
    z_local = pltpu.make_async_copy(z4_hbm, z4, l_sem.at[2])
    x_local = pltpu.make_async_copy(x0_hbm, feature.at[0], l_sem.at[3])
    for copy in d_local:
        copy.start()
    h_local.start()

    def w_copy(q, act):
        layer, slot = 1 - q // 3, q % 2
        three = pl.ds(q % 3 * 3, 3)
        whole = w_hbm.at[0].reshape(9, 2 * half, 2 * half)

        @pl.when(layer == section)
        def _():
            src = whole.at[three, mine(half)]
            act(pltpu.make_async_copy(src, wstage.at[slot], w_sem.at[slot]))

        @pl.when(layer != section)
        def _():
            act(pltpu.make_async_copy(wr_hbm.at[three], wstage.at[slot], w_sem.at[slot]))

    for k in range(3):
        clear_margins(fd.at[k], items, pitch)
    for k in range(3):
        clear_edges(taps.at[k])

    def d_remote(k):
        src = d5_hbm if k == 0 else fd.at[0, :, pl.ds(HEAD, pitch)]
        return pltpu.make_async_remote_copy(
            src, fd.at[1 + k, :, pl.ds(HEAD, pitch)],
            d_sem.at[k, 0], d_sem.at[k, 1], device_id=partner, device_id_type=MESH,
        )

    real = lax.broadcasted_iota(jnp.int32, (pitch, half), 0) < items * SIDE

    def column_sums():
        def add(row, total):
            v = fd[0, row, pl.ds(HEAD, pitch)]
            return total + jnp.sum(v.reshape(pitch // 8, 8, half), axis=0)

        return jnp.sum(lax.fori_loop(0, SIDE, add, jnp.zeros((8, half), F32)), axis=0, keepdims=True)

    for copy, span in zip(d_local, PARTS):
        copy.wait()
        build_taps(fd.at[0], taps.at[0], items, pitch, span=span)
    pl.semaphore_wait(barrier, 5 + (z + 1) // 2 % 2 if reduce else 1)
    d_remote(0).start()
    w_copy(0, lambda copy: copy.start())
    z_local.start()
    x_local.start()
    acc[...] = jnp.zeros_like(acc)
    h_local.wait()

    def first_sums():
        b_send[0, 0:8] = jnp.broadcast_to(column_sums(), (8, half))

    def enter(layer):
        z_local.wait()
        x_local.wait()

        @pl.loop(0, SIDE)
        def _(row):
            v = z4[row]
            s = sigmoid(v)
            d = acc[row] * (s * (1.0 + v * (1.0 - s)))
            fd[0, row, pl.ds(HEAD, pitch)] = jnp.where(real, d, 0.0)

        d_remote(1).start()
        build_taps(fd.at[0], taps.at[2], items, pitch)
        which = lax.broadcasted_iota(jnp.int32, (8, half), 0) == 0
        b_send[0] = jnp.where(which, jnp.broadcast_to(column_sums(), (8, half)), b_send[0])
        acc[...] = jnp.zeros_like(acc)

    def receive(k):
        d_remote(k).wait_recv()
        build_taps(fd.at[1 + k], taps.at[1], items, pitch)

    def kernel_unit(n):
        layer, step = 1 - n // units, n % units
        t, m = step // 2, step % 2
        row, col = 2 - t // 3, 2 - t % 3
        terms = ((0, 0), (1, 0), (0, 1))

        def contract(first, count):
            size = count * pitch
            v = [
                feature[layer, m, term, pl.ds(first, count)].reshape(size, half) for term in range(2)
            ]
            d = [
                taps[2 - 2 * layer, col, term, pl.ds(first + row, count)].reshape(size, half) for term in range(2)
            ]
            tail = size % 256
            cut = size - tail
            total = None
            for a, b in terms:
                part = dot_tn(v[a][:cut], d[b][:cut])
                total = part if total is None else total + part
            if tail:
                total += dot_tn(
                    jnp.concatenate([v[a][cut:] for a, b in terms], 0),
                    jnp.concatenate([d[b][cut:] for a, b in terms], 0),
                )
            own[n % RING] = total

        pl.when(row == 1)(lambda: contract(0, SIDE))
        pl.when(row != 1)(lambda: contract(jnp.where(row == 0, 1, 0), SIDE - 1))

    def input_piece(layer, p):
        g, j = p // 6, p % 6
        q = 3 * (1 - layer) + g

        @pl.when(j == 0)
        def _():
            w_copy(q, lambda copy: copy.wait())
            pl.when(q + 1 < 6)(lambda: w_copy(q + 1, lambda copy: copy.start()))
            for k in range(3):
                wbf[0, k], wbf[1, k] = split(wstage[q % 2, k])

        def tile(start, count):
            total = None
            for h in range(2):
                for k in range(3):
                    for a, b in ((0, 0), (1, 0), (0, 1)):
                        v = taps[1 if h else 2 - 2 * layer, 2 - k, a, pl.ds(start + 2 - g, count)]
                        w = wbf[b, k, :, pl.ds(pl.multiple_of((section + h) % 2 * half, half), half)]
                        part = dot_nt(v.reshape(count * pitch, half), w)
                        total = part if total is None else total + part
            acc[pl.ds(start, count)] += total.reshape(count, pitch, half)

        top, bottom = (j == 0) & (g == 2), (j == 5) & (g == 0)
        pl.when((j < 5) & jnp.logical_not(top))(lambda: tile(2 * j, 2))
        pl.when(top)(lambda: tile(1, 1))
        pl.when((j == 5) & (g != 0))(lambda: tile(10, SIDE - 10))
        pl.when(bottom)(lambda: tile(10, SIDE - 11))

    def bias_copy(k, device):
        return pltpu.make_async_remote_copy(
            b_send.at[k], b_recv.at[k], bs_sem.at[k], br_sem.at[k], device_id=device, device_id_type=MESH
        )

    put_row = pltpu.make_async_copy(b_row, bg_out, bo_sem.at[0])

    def bias_step(k):
        if k > 0 and k < 5:
            bias_copy(k - 1, pairs[k - 1]).wait_recv()
            b_send[k] = b_send[k - 1] + b_recv[k - 1]
        if k < 4:
            bias_copy(k, pairs[k]).start()
        if k == 4:
            bias_copy(4, partner).start()
        if k == 5:
            bias_copy(4, partner).wait_recv()
            for s in range(2):

                @pl.when(section == s)
                def _(s=s):
                    b_row[:, s * half : (s + 1) * half] = b_send[4, s : s + 1]
                    b_row[:, (1 - s) * half : (2 - s) * half] = b_recv[4, s : s + 1]

            put_row.start()

    tiles = half // LANES
    put_acc = [
        pltpu.make_async_copy(
            acc.at[:, :, pl.ds(tile * LANES, LANES)], gin_out.at[tile], l_sem.at[4 + tile]
        )
        for tile in range(tiles)
    ]

    def local_part(n):
        layer, row0 = 1 - n // units, n % units * half
        dst = gx_out.at[layer, pl.ds(pl.multiple_of(row0, half), half)]
        return pltpu.make_async_copy(own.at[n % RING], dst, sems[0].at[n % RING])

    def service(u, odd):
        for k, offset in enumerate(OFFSETS):
            if k == 0 or offset % 2 != odd:
                continue
            valid, n = unit_of(u - offset // 2)

            @pl.when(valid)
            def _():
                stages = exchange(n, own, r_first, r_line, r_last, fin, gx_out, wg_out, sems)
                stages[k]()

    lag = LAG
    turn = lag + STEPS
    late0 = turn + lag
    last = 2 * units + (OFFSETS[-1] + 1) // 2

    def unit_of(u):
        return (u >= 0) & (u < 2 * units), u

    @pl.loop(0, last)
    def _(u):
        valid, n = unit_of(u)
        pl.when(u == lag)(lambda: receive(0))
        pl.when(u == 2)(lambda: first_sums())
        pl.when(u == turn)(lambda: enter(0))
        pl.when(u == late0)(lambda: receive(1))

        @pl.when(valid)
        def _():
            if not reduce:
                pl.when(n >= RING)(lambda: local_part(n - RING).wait())
            kernel_unit(n)
            if reduce:
                exchange(n, own, r_first, r_line, r_last, fin, gx_out, wg_out, sems)[0]()
            else:
                local_part(n).start()

        if reduce:
            service(u, 0)
        early = (u >= lag) & (u < turn)
        late = (u >= late0) & (u < late0 + units)

        done = jnp.where(early, lax.div((u - lag) * units, STEPS), u - late0)
        upto = jnp.where(early, lax.div((u - lag + 1) * units, STEPS), done + 1)

        @pl.loop(0, jnp.where(early | late, upto - done, 0))
        def _(i):
            input_piece(jnp.where(early, 1, 0), done + i)

        @pl.when(u == late0 + units - 1)
        def _():
            for copy in put_acc:
                copy.start()

        if reduce:
            service(u, 1)
        for k in range(6 if reduce else 0):
            pl.when(u == turn + 2 + 2 * k)(lambda k=k: bias_step(k))

    if not reduce:

        @pl.loop(2 * units - RING, 2 * units)
        def _(n):
            local_part(n).wait()

    if reduce:
        for k in range(5):
            bias_copy(k, (pairs + [partner])[k]).wait_send()
        put_row.wait()
    else:
        put_sums = pltpu.make_async_copy(b_send.at[0], bg_out, bo_sem.at[0])
        put_sums.start()
        put_sums.wait()
    for k in range(2):
        d_remote(k).wait_send()
    for copy in put_acc:
        copy.wait()


def backward(d5, z4, h0, x0, weights, rows_other, items, reduce):
    maps = d5.shape
    _, pitch, half = maps
    channels = 2 * half
    any_spec = pl.BlockSpec(memory_space=pl.ANY)
    dma = pltpu.SemaphoreType.DMA
    shape = jax.ShapeDtypeStruct
    ring = RING
    part, chunk = half // 2, half // 8
    return pl.pallas_call(
        functools.partial(backward_kernel, items, pitch, reduce),
        name="backward",
        out_shape=[
            shape((half // LANES, SIDE, pitch, LANES), F32),
            shape((2, 9 * channels, half), F32),
            shape((9 * channels, channels), F32),
            shape((1, channels) if reduce else (8, half), F32),
        ],
        in_specs=[any_spec] * 6,
        out_specs=[any_spec] * 4,
        scratch_shapes=[
            pltpu.VMEM((3, SIDE, HEAD + pitch + HEAD, half), F32),
            pltpu.VMEM((3, 3, 2, SIDE + 2, pitch, half), BF16),
            pltpu.VMEM((2, 2, 2) + maps, BF16),
            pltpu.VMEM(maps, F32),
            pltpu.VMEM(maps, F32),
            pltpu.VMEM((2, 3, half, channels), F32),
            pltpu.VMEM((2, 3, half, channels), BF16),
            pltpu.VMEM((ring, half, half), F32),
            pltpu.VMEM((ring, part, half), F32),
            pltpu.VMEM((ring, 2, part, half), F32),
            pltpu.VMEM((ring, chunk, half), F32),
            pltpu.VMEM((ring, chunk, half), F32),
            pltpu.VMEM((5, 8, half), F32),
            pltpu.VMEM((5, 8, half), F32),
            pltpu.VMEM((1, channels), F32),
            dma((4 + half // LANES,)), dma((len(PARTS),)), dma((2,)), dma((2, 2)), dma((5,)), dma((5,)), dma((1,)),
            dma((ring,)), dma((ring,)), dma((ring, 2)), dma((ring,)), dma((ring, 2)), dma((ring,)),
            dma((ring,)), dma((ring,)),
        ],
        compiler_params=pltpu.CompilerParams(
            collective_id=1, has_side_effects=True, vmem_limit_bytes=62 * 2**20
        ),
    )(d5, z4, h0, x0, weights, rows_other)


def finish_kernel(
    items, rows_in, act_hbm, gin_hbm, wg_hbm, bias_hbm, act_out, gin_out, wg_out, bias_out,
    act_rows, gin_rows, act, gin, wg, bias, i_sem, o_sem,
):
    pieces = wg.shape[0] // rows_in
    count = pieces + 3

    def incoming(k):
        if k < 2:
            src, dst = ((act_hbm, act_rows), (gin_hbm, gin_rows))[k]
        elif k == count - 1:
            src, dst = bias_hbm, bias
        else:
            rows = pl.ds((k - 2) * rows_in, rows_in)
            src, dst = wg_hbm.at[rows], wg.at[rows]
        return pltpu.make_async_copy(src, dst, i_sem.at[k])

    def outgoing(k):
        if k < 2:
            src, dst = ((act, act_out), (gin, gin_out))[k]
        elif k == count - 1:
            src, dst = bias, bias_out
        else:
            rows = pl.ds((k - 2) * rows_in, rows_in)
            src, dst = wg.at[rows], wg_out.at[0, rows]
        return pltpu.make_async_copy(src, dst, o_sem.at[k])

    for k in range(count):
        incoming(k).start()
    for k, (rows, maps) in enumerate(((act_rows, act), (gin_rows, gin))):
        incoming(k).wait()
        for row in range(SIDE):
            for n in range(items):
                for tile in range(rows.shape[0]):
                    maps[
                        n, row * SIDE : (row + 1) * SIDE, tile * LANES : (tile + 1) * LANES
                    ] = rows[tile, row, pl.ds(n, SIDE, stride=items), :]
        outgoing(k).start()
        for j in range(pieces):
            if j % 2 == k:
                incoming(2 + j).wait()
                outgoing(2 + j).start()
    incoming(count - 1).wait()
    outgoing(count - 1).start()
    for k in range(count):
        outgoing(k).wait()


def finish(act, gin, wg, bias, items):
    half = act.shape[0] * LANES
    any_spec = pl.BlockSpec(memory_space=pl.ANY)
    maps = (items, SIDE * SIDE, half)
    pieces = 6
    dma = pltpu.SemaphoreType.DMA
    return pl.pallas_call(
        functools.partial(finish_kernel, items, wg.shape[0] // pieces),
        name="finish",
        out_shape=[
            jax.ShapeDtypeStruct(maps, F32),
            jax.ShapeDtypeStruct(maps, F32),
            jax.ShapeDtypeStruct((1,) + wg.shape, F32),
            jax.ShapeDtypeStruct(bias.shape, F32),
        ],
        in_specs=[any_spec] * 4,
        out_specs=[any_spec] * 4,
        scratch_shapes=[
            pltpu.VMEM(act.shape, F32),
            pltpu.VMEM(act.shape, F32),
            pltpu.VMEM(maps, F32),
            pltpu.VMEM(maps, F32),
            pltpu.VMEM(wg.shape, F32),
            pltpu.VMEM(bias.shape, F32),
            dma((pieces + 3,)),
            dma((pieces + 3,)),
        ],
        compiler_params=pltpu.CompilerParams(vmem_limit_bytes=62 * 2**20),
    )(act, gin, wg, bias)


def per_device(flow_maps, weights, biases, stack_lengths, grad_seeds):
    items = flow_maps.shape[0]
    channels = flow_maps.shape[2]
    half = channels // 2
    pitch = ceil_to(items * SIDE, 16)
    section = lax.axis_index("section")
    act, z4, d5, h0, x0, rows_other = forward(
        flow_maps, weights, biases, grad_seeds, stack_lengths, items, pitch
    )
    fused = lax.axis_size("dp") == 16
    gin, parts, grad, bias = backward(d5, z4, h0, x0, weights, rows_other, items, fused)
    if not fused:
        parts, bias = lax.psum((parts, bias[:2]), "dp")
        given = lax.dynamic_index_in_dim(parts, 1 - section, 0, keepdims=False)
        kept = lax.dynamic_index_in_dim(parts, section, 0, keepdims=False)
        got = lax.ppermute(given, "section", [(0, 1), (1, 0)])
        first, second = jnp.where(section == 0, kept, got), jnp.where(section == 0, got, kept)
        grad = jnp.concatenate([first, second], axis=1)
        both = lax.all_gather(bias, "section", axis=1, tiled=True)
        bias = lax.dynamic_index_in_dim(both, section, 0)
    act, gin, grad, bias = finish(act, gin, grad, bias, items)
    return (act, gin, grad, bias)


def solution(mesh):
    in_specs = (P("dp", None, None), P("section", None, None), P("section", None), P("dp"), P("dp"))
    out_specs = (
        P("dp", None, "section"),
        P("dp", None, "section"),
        P("section", None, None),
        P("section", None),
    )
    return jax.shard_map(
        per_device, mesh=mesh, in_specs=in_specs, out_specs=out_specs, check_vma=False
    )
```
